256 devices in a mesh: dp: 8 (over z), seq: 32 (over y, x, core).
Axes of the slice: x: 4, y: 4, z: 8, core: 2. Of those that a mesh axis runs over, the one named last changes fastest.
Arguments:
- queries: bfloat16 [32768, 12288], P(('dp', 'seq')), may hold values from -204 to 204
- kv_latent: bfloat16 [32768, 512], P(('dp', 'seq')), may hold values from -6 to 6
- key_rope: bfloat16 [32768, 64], P(('dp', 'seq')), may hold values from -6 to 6
- kv_gain: float32 [512], replicated, may hold values from 0.1 to 1.9
- kv_up: bfloat16 [512, 16384], P(None, 'seq'), may hold values from -0.25 to 0.25
- segment_blocks: int32 [8], replicated, may hold values from 1 to 8, 32 in all
- bucket_of: int32 [8], replicated, may hold values from 0 to 7, each once
- doc_breaks: int32 [8, 32], replicated, may hold values from 0 to 1, as said below
Outputs:
- attended: bfloat16 [32768, 8192], P(('dp', 'seq'))
The draws below stay inside these ranges and needn't reach their ends.
Inputs may be any that keep to these rules, and one draw needn't show every extreme that they name: The plan: rollout s's tiles are cut in order into segments of segment_blocks[g] tiles, segment g goes to bucket bucket_of[(s + g) mod 8]. The entries sum to 32, and the largest is exactly 8. `bucket_of`: each bucket number appears once. `doc_breaks`: 1 marks a tile of a rollout where a new document begins; a document also begins at every segment's first tile. Some rollout has no mark and some rollout has every tile marked.
All inputs are finite; a program needn't handle non-finite values.
Results may differ from the reference program's by a relative error of at most 0.012.
The reference program's roundings to bfloat16 on the way (of `normed`, `keyval` and `weights`) count: a program that leaves them out, or rounds other values in their place, can miss the bound.
Values may be sent and summed in bfloat16 or wider, within the bound.
A program may use at most 128 MiB of HBM per device.

```python
import math
import jax
import jax.numpy as jnp
import numpy as np
from jax import lax

H = 64
HD_NOPE = 128
HD_ROPE = 64
HD_V = 128
LAT = 512
BLK = 128
NBLK = 32
WIN = 4096
TOKENS = 32768
SEG_MOST = 8
N_DP = 8


def draw_queries(key, part):
    key = jax.random.fold_in(key, 11)
    shape = (TOKENS, H * (HD_NOPE + HD_ROPE))
    return jnp.clip(jax.random.normal(key, shape, jnp.float32), -5.0, 5.0).astype(jnp.bfloat16)


def draw_doc_breaks(key, part):
    key = jax.random.fold_in(key, 5)
    rates = jax.random.randint(jax.random.fold_in(key, 1), (N_DP, 1), 0, 5)
    order = jax.random.permutation(jax.random.fold_in(key, 2), N_DP)
    rates = rates.at[order[0]].set(4).at[order[1]].set(0)
    tosses = jax.random.randint(jax.random.fold_in(key, 3), (N_DP, NBLK), 0, 4)
    return (tosses < rates).astype(jnp.int32)


def levels(own_key, extent, split, least, top_value):
    def one(dim, shards_of):
        draws = jax.random.uniform(jax.random.fold_in(jax.random.fold_in(own_key, 6), dim), (shards_of,), jnp.float32, least / len(split), top_value / len(split))
        return jnp.repeat(jnp.exp(draws), extent[dim] // shards_of).reshape((-1,) + (1,) * (len(extent) - dim - 1))

    gain = one(*split[0])
    for cut in split[1:]:
        gain = gain * one(*cut)
    return gain


def profile(count, total, bound, skew):
    loads = [(1 << 20) // math.isqrt(grade ** skew) + 1 for grade in range(2, count + 1)]
    rest, counts = total - bound - (count - 1), [1] * (count - 1)
    while rest > 0:
        free = [i for i in range(count - 1) if counts[i] < bound]
        whole, budget = sum([loads[i] for i in free]), rest
        for i in free:
            extra = min(bound - counts[i], max(1, budget * loads[i] // whole), rest)
            counts[i] = counts[i] + extra
            rest = rest - extra
    return np.array([bound] + counts)


def uneven(stream_key, count, total, bound, slope):
    if count == 2:
        one = jax.random.randint(stream_key, (), max(1, total - bound), min(bound, total - 1) + 1)
        return jnp.stack([one, total - one])
    sizes = jnp.asarray(profile(count, total, bound, slope), jnp.int32)
    pairs = (count - 1) // 2
    giver, receiver = sizes[1:1 + 2 * pairs:2], sizes[2:2 + 2 * pairs:2]
    slack = jnp.minimum(giver - 1, bound - receiver)
    shifted = jax.random.randint(jax.random.fold_in(stream_key, 1), (pairs,), 0, 1 << 20) % (slack + 1)
    sizes = sizes.at[1:1 + 2 * pairs:2].set(giver - shifted).at[2:2 + 2 * pairs:2].set(receiver + shifted)
    return sizes[jax.random.permutation(jax.random.fold_in(stream_key, 2), count)]


def gaussian(stream_key, dims, width, bound, pieces=(), kind=jnp.bfloat16):
    factor_of = levels(stream_key, dims, pieces, -0.22, 0.18) if pieces else 1.0
    drawn = jax.random.normal(stream_key, dims, jnp.float32) * width * factor_of
    return jnp.minimum(jnp.maximum(drawn, -bound), bound).astype(kind)


def setup_inputs(seed: int = 0) -> dict:
    seeds = jax.random.split(jax.random.key(seed), 9)
    queries = draw_queries(jax.random.fold_in(seeds[8], 71), 0)
    kv_latent = gaussian(seeds[1], (TOKENS, LAT), 1.0, 6.0, ((0, 256),))
    key_rope = gaussian(seeds[2], (TOKENS, HD_ROPE), 1.0, 6.0, ((0, 256),))
    kv_gain = jnp.clip(1.0 + 0.18 * jax.random.normal(seeds[3], (LAT,), jnp.float32), 0.1, 1.9)
    kv_up = gaussian(seeds[4], (LAT, H * (HD_NOPE + HD_V)), LAT ** -0.5, 0.25, ((1, 32),))
    segment_blocks = uneven(seeds[5], N_DP, NBLK, SEG_MOST, 1).astype(jnp.int32)
    bucket_of = jax.random.permutation(seeds[6], N_DP).astype(jnp.int32)
    doc_breaks = draw_doc_breaks(jax.random.fold_in(seeds[8], 71), 0)
    return dict(queries=queries, kv_latent=kv_latent, key_rope=key_rope, kv_gain=kv_gain, kv_up=kv_up, segment_blocks=segment_blocks, bucket_of=bucket_of, doc_breaks=doc_breaks)


epsilon = 1e-06
row_block = 512

def inverse_of(bucket_of):
    slot_count = bucket_of.shape[0]
    indices = jnp.arange(slot_count, dtype=jnp.int32)
    return lax.optimization_barrier(jnp.sum(jnp.where(bucket_of[:, None] == indices[None, :], indices[:, None], 0), axis=0)).astype(jnp.int32)

def segment_starts(segment_blocks):
    return (jnp.cumsum(segment_blocks) - segment_blocks).astype(jnp.int32)

def bucket_layout(segment_blocks, bucket_of, bucket, count_blocks):
    slot_count = segment_blocks.shape[0]
    indices = jnp.arange(slot_count, dtype=jnp.int32)
    starts = segment_starts(segment_blocks)
    segment_of = (inverse_of(bucket_of)[bucket] - indices) % slot_count
    lengths = segment_blocks[segment_of]
    place_end = jnp.cumsum(lengths).astype(jnp.int32)
    place_start = place_end - lengths
    block_ids = jnp.arange(count_blocks, dtype=jnp.int32)
    source = lax.optimization_barrier(jnp.sum((place_end[None, :] <= block_ids[:, None]).astype(jnp.int32), axis=1))
    within = block_ids - place_start[source]
    return (source, within, starts[segment_of[source]] + within)

def first_blocks(starts_here):
    block_ids = jnp.arange(starts_here.shape[0], dtype=jnp.int32)
    return lax.cummax(jnp.where(starts_here, block_ids, 0), axis=0)

def attend(query_heads, key_heads, value_heads, first_row):
    tile_rows = min(row_block, WIN)
    lead_rows = (SEG_MOST - 1) * BLK
    score_scale = (HD_NOPE + HD_ROPE) ** (-0.5)
    key_pad = jnp.pad(key_heads, ((lead_rows, 0), (0, 0), (0, 0)))
    value_pad = jnp.pad(value_heads, ((lead_rows, 0), (0, 0), (0, 0)))

    def one_block(position):
        first_query = position * tile_rows
        query_tile = lax.dynamic_slice_in_dim(query_heads, first_query, tile_rows, 0).astype(jnp.float32)
        key_tile = lax.dynamic_slice_in_dim(key_pad, first_query, tile_rows + lead_rows, 0).astype(jnp.float32)
        value_tile = lax.dynamic_slice_in_dim(value_pad, first_query, tile_rows + lead_rows, 0).astype(jnp.float32)
        query_pos = first_query + jnp.arange(tile_rows, dtype=jnp.int32)
        key_pos = first_query - lead_rows + jnp.arange(tile_rows + lead_rows, dtype=jnp.int32)
        doc_firsts = lax.dynamic_slice_in_dim(first_row, first_query, tile_rows, 0)
        allowed = (key_pos[None, :] <= query_pos[:, None]) & (key_pos[None, :] >= doc_firsts[:, None])
        scores = jnp.einsum('qhe,khe->hqk', query_tile, key_tile) * score_scale
        scores = jnp.where(allowed[None, :, :], scores, jnp.float32(-1e+30))
        row_max = lax.optimization_barrier(jnp.max(scores, axis=2, keepdims=True))
        exponent = jnp.exp(scores - row_max)
        weights = (exponent / lax.optimization_barrier(jnp.sum(exponent, axis=2, keepdims=True))).astype(jnp.bfloat16)
        weights = lax.optimization_barrier(weights)
        attended = jnp.einsum('hqk,khe->qhe', weights.astype(jnp.float32), value_tile)
        return attended.reshape(tile_rows, H * HD_V).astype(jnp.bfloat16)
    return lax.map(one_block, jnp.arange(WIN // tile_rows, dtype=jnp.int32)).reshape(WIN, H * HD_V)

def reference(queries, kv_latent, key_rope, kv_gain, kv_up, segment_blocks, bucket_of, doc_breaks):

    def one_bucket(bucket):
        source, within, src_block = bucket_layout(segment_blocks, bucket_of, bucket, NBLK)
        starts_here = (within == 0) | (doc_breaks[source, src_block] == 1)
        first_row = jnp.repeat(first_blocks(starts_here) * BLK, BLK)
        row_ids = ((source * NBLK + src_block)[:, None] * BLK + jnp.arange(BLK, dtype=jnp.int32)[None, :]).reshape(-1)
        query_heads = jnp.take(queries, row_ids, axis=0).reshape(WIN, H, HD_NOPE + HD_ROPE)
        latent_wide = jnp.take(kv_latent, row_ids, axis=0).astype(jnp.float32)
        rotary = jnp.take(key_rope, row_ids, axis=0)
        normed = (latent_wide * lax.rsqrt(lax.optimization_barrier(jnp.mean(latent_wide * latent_wide, axis=1, keepdims=True)) + epsilon) * kv_gain).astype(jnp.bfloat16)
        keyval = jnp.dot(normed, kv_up, preferred_element_type=jnp.float32).astype(jnp.bfloat16)
        keyval = keyval.reshape(WIN, H, HD_NOPE + HD_V)
        key_heads = jnp.concatenate([keyval[:, :, :HD_NOPE], jnp.broadcast_to(rotary[:, None, :], (WIN, H, HD_ROPE))], axis=2)
        return attend(query_heads, key_heads, keyval[:, :, HD_NOPE:], first_row)
    return lax.map(one_bucket, jnp.arange(N_DP, dtype=jnp.int32)).reshape(TOKENS, H * HD_V)
```

```python
import functools
import math

import jax
import jax.numpy as jnp
from jax import lax
from jax.experimental import pallas as pl
from jax.experimental.pallas import tpu as pltpu
from jax.sharding import PartitionSpec as P

HD_NOPE = 128
HD_ROPE = 64
HD_V = 128
BLK = 128
LAT = 512
NBLK = 32
N_DP = 8
SEG_MOST = 8
NY, NX, NC = 4, 4, 2
N_SEQ = NY * NX * NC
LEAD = (SEG_MOST - 1) * BLK
KEYS = LEAD + 2 * BLK
XW = LAT + 2 * HD_ROPE
EPS = 1e-06
NEG = -1e30
EXP_SCALE = (HD_NOPE + HD_ROPE) ** -0.5 * math.log2(math.e)
HALF = BLK // 2


def seq_peer(y, x, c, o):
    dc, dx, dy = o % NC, (o // NC) % NX, o // (NC * NX)
    return ((y + dy) % NY) * (NX * NC) + ((x + dx) % NX) * NC + (c + dc) % NC


def seq_source(y, x, c, o):
    dc, dx, dy = o % NC, (o // NC) % NX, o // (NC * NX)
    return ((y + NY - dy) % NY) * (NX * NC) + ((x + NX - dx) % NX) * NC + (c + NC - dc) % NC


def kernel(
    queries, latent, rope2, gain, kv_up, seg, bucket_of, breaks,
    out,
    xall, qa, qb, wts, kext, vext, att, zsend, zrecv0, zrecv1, osend,
    starts_sm, first_sm, pick_sm, slot_sm,
    l1_send, l1_recv, l2_send, l2_recv, sib_send, sib_recv,
    q_send, q_recv, z_send, z_recv, o_send, o_recv, own_sem,
):
    s = lax.axis_index("dp")
    me = lax.axis_index("seq")
    y, x, c = me // (NX * NC), (me // NC) % NX, me % NC

    def remote(src, dst, send, recv, **axes):
        return pltpu.make_async_remote_copy(
            src_ref=src, dst_ref=dst, send_sem=send, recv_sem=recv,
            device_id=axes, device_id_type=pl.DeviceIdType.MESH,
        )

    zrecv = (zrecv0, zrecv1)

    barrier = pltpu.get_barrier_semaphore()

    def greet_seq(o, carry):
        pl.semaphore_signal(barrier, inc=1, device_id={"seq": seq_peer(y, x, c, o)},
                            device_id_type=pl.DeviceIdType.MESH)
        return carry

    lax.fori_loop(1, N_SEQ, greet_seq, 0)
    for d in range(1, N_DP):
        pl.semaphore_signal(barrier, inc=1, device_id={"dp": (s + d) % N_DP},
                            device_id_type=pl.DeviceIdType.MESH)

    lat = latent[...].astype(jnp.float32)
    normed = (
        lat * lax.rsqrt(jnp.mean(lat * lat, axis=1, keepdims=True) + EPS) * gain[...]
    ).astype(jnp.bfloat16)
    rows = jnp.concatenate([normed, rope2[...]], axis=1).reshape(2, HALF, XW)
    xall[y, x, c] = rows

    pl.semaphore_wait(barrier, N_SEQ - 1 + N_DP - 1)

    def at_x(d):
        return y * (NX * NC) + ((x + d) % NX) * NC + c

    def at_y(d):
        return ((y + d) % NY) * (NX * NC) + x * NC + c

    sibling = y * (NX * NC) + x * NC + (1 - c)
    ph1 = []
    for d in range(1, 4):
        own_a, own_b = xall.at[y, x, c, 0], xall.at[y, x, c, 1]
        ph1.append(remote(own_a, own_a, l1_send.at[0, d], l1_recv.at[0, d], seq=at_x(d)))
        ph1.append(remote(own_b, own_b, l1_send.at[1, d], l1_recv.at[1, d], seq=at_y(d)))
    for cp in ph1:
        cp.start()

    def q_copy(o, part, peer, slot):
        width = 2 * BLK if part == 0 else BLK
        begin = pl.multiple_of(peer * (3 * BLK) + part * 2 * BLK, BLK)
        dst = (qa if part == 0 else qb).at[slot]
        return remote(queries.at[:, pl.ds(begin, width)], dst,
                      q_send.at[part, o], q_recv.at[part, o], seq=peer)

    def q_start(part, lo, hi):
        def body(o, carry):
            q_copy(o, part, seq_peer(y, x, c, o), me).start()
            return carry
        lax.fori_loop(lo, hi, body, 0)

    def q_arrive(part):
        def body(o, carry):
            q_copy(o, part, seq_peer(y, x, c, o), seq_source(y, x, c, o)).wait_recv()
            return carry
        lax.fori_loop(1, N_SEQ, body, 0)

    def q_drain(part):
        def body(o, carry):
            q_copy(o, part, seq_peer(y, x, c, o), me).wait_send()
            return carry
        lax.fori_loop(1, N_SEQ, body, 0)

    def q_own(part):
        width = 2 * BLK if part == 0 else BLK
        begin = pl.multiple_of(me * (3 * BLK) + part * 2 * BLK, BLK)
        return pltpu.make_async_copy(queries.at[:, pl.ds(begin, width)],
                                     (qa if part == 0 else qb).at[me], own_sem.at[part])

    q_own(0).start()
    q_own(1).start()

    for d in range(1, 4):
        there = xall.at[y, (x + NX - d) % NX, c, 0]
        remote(there, there, l1_send.at[0, d], l1_recv.at[0, d], seq=at_x(d)).wait_recv()
    row_a = xall.at[y, :, c, 0]
    ph2 = [remote(row_a, row_a, l2_send.at[0, d], l2_recv.at[0, d], seq=at_y(d)) for d in range(1, 4)]
    for cp in ph2:
        cp.start()
    for d in range(1, 4):
        there = xall.at[(y + NY - d) % NY, x, c, 1]
        remote(there, there, l1_send.at[1, d], l1_recv.at[1, d], seq=at_y(d)).wait_recv()
    col_b = xall.at[:, x, c, 1]
    ph2b = [remote(col_b, col_b, l2_send.at[1, d], l2_recv.at[1, d], seq=at_x(d)) for d in range(1, 4)]
    for cp in ph2b:
        cp.start()
    sib = [
        remote(row_a, row_a, sib_send.at[0, 0], sib_recv.at[0, 0], seq=sibling),
        remote(col_b, col_b, sib_send.at[1, 0], sib_recv.at[1, 0], seq=sibling),
    ]
    for cp in sib:
        cp.start()

    q_start(0, 1, N_SEQ)
    q_start(1, 1, N_SEQ)

    total = jnp.int32(0)
    start_of = []
    for g in range(N_DP):
        start_of.append(total)
        starts_sm[g] = total
        total = total + seg[g]
    mine = jnp.int32(0)
    for j in range(N_DP):
        mine = mine + jnp.where(bucket_of[j] == s, j, 0)
    for d in range(N_DP):
        b = (s + d) % N_DP
        at = jnp.int32(0)
        for j in range(N_DP):
            at = at + jnp.where(bucket_of[j] == b, j, 0)
        slot_sm[d] = starts_sm[(at - s + N_DP) % N_DP]
    ends, begins = [], []
    total = jnp.int32(0)
    for r in range(N_DP):
        begins.append(total)
        total = total + seg[(mine - r + N_DP) % N_DP]
        ends.append(total)

    def plan_tile(k, first):
        begins_here = breaks[s, k] == 1
        pick = jnp.int32(0)
        for r in range(N_DP):
            begins_here = begins_here | (start_of[r] == k)
            inside = (k >= begins[r]) & (k < ends[r])
            pick = pick + jnp.where(inside, r * SEG_MOST + k - begins[r], 0)
        first = jnp.where(begins_here, k, first)
        first_sm[k] = first
        pick_sm[k] = pick
        return first

    lax.fori_loop(0, NBLK, plan_tile, jnp.int32(0))

    lane = lax.broadcasted_iota(jnp.int32, (LAT, BLK), 1)
    wts[:, : 2 * BLK] = kv_up[:, : 2 * BLK]
    turned = pltpu.roll(kv_up[:, 2 * BLK : 3 * BLK].astype(jnp.float32), HALF, 1)
    wts[:, 2 * BLK : 3 * BLK] = jnp.where(lane < HALF, 0.0, turned).astype(jnp.bfloat16)
    wts[:, 3 * BLK : 4 * BLK] = jnp.where(lane < HALF, turned, 0.0).astype(jnp.bfloat16)
    wts[:, 4 * BLK :] = kv_up[:, 3 * BLK :]
    kext[:, :LEAD, :] = jnp.zeros((2, LEAD, 2 * BLK), jnp.bfloat16)
    vext[:, :LEAD, :] = jnp.zeros((2, LEAD, 2 * BLK), jnp.bfloat16)

    for d in range(1, 4):
        got = xall.at[(y + NY - d) % NY, :, c, 0]
        remote(got, got, l2_send.at[0, d], l2_recv.at[0, d], seq=at_y(d)).wait_recv()
        sib.append(remote(got, got, sib_send.at[0, d], sib_recv.at[0, d], seq=sibling))
        sib[-1].start()
        got = xall.at[:, (x + NX - d) % NX, c, 1]
        remote(got, got, l2_send.at[1, d], l2_recv.at[1, d], seq=at_x(d)).wait_recv()
        sib.append(remote(got, got, sib_send.at[1, d], sib_recv.at[1, d], seq=sibling))
        sib[-1].start()
    for d in range(4):
        got = xall.at[(y + NY - d) % NY, :, 1 - c, 0]
        remote(got, got, sib_send.at[0, d], sib_recv.at[0, d], seq=sibling).wait_recv()
        got = xall.at[:, (x + NX - d) % NX, 1 - c, 1]
        remote(got, got, sib_send.at[1, d], sib_recv.at[1, d], seq=sibling).wait_recv()

    lane2 = lax.broadcasted_iota(jnp.int32, (2 * BLK, BLK), 1)

    def project(i, carry):
        block = xall[i // NX, i % NX].reshape(2 * BLK, XW)
        rot = block[:, LAT:].astype(jnp.float32)
        kv = jnp.dot(block[:, :LAT], wts[...], preferred_element_type=jnp.float32)
        at = pl.ds(pl.multiple_of(LEAD + i * 2 * BLK, BLK), 2 * BLK)
        ones = jnp.ones((2 * BLK, BLK), jnp.bfloat16)
        kext[0, at, :BLK] = kv[:, :BLK].astype(jnp.bfloat16)
        kext[0, at, BLK:] = jnp.where(lane2 < HALF, rot, 0.0).astype(jnp.bfloat16)
        vext[0, at, :BLK] = kv[:, BLK : 2 * BLK].astype(jnp.bfloat16)
        vext[0, at, BLK:] = ones
        kext[1, at, :BLK] = kv[:, 2 * BLK : 3 * BLK].astype(jnp.bfloat16)
        kext[1, at, BLK:] = jnp.where(lane2 < HALF, kv[:, 3 * BLK : 4 * BLK], rot).astype(jnp.bfloat16)
        vext[1, at, :BLK] = kv[:, 4 * BLK :].astype(jnp.bfloat16)
        vext[1, at, BLK:] = ones
        return carry

    lax.fori_loop(0, NBLK // 2, project, 0)

    row_id = lax.broadcasted_iota(jnp.int32, (BLK, BLK), 0)
    col_id = lax.broadcasted_iota(jnp.int32, (BLK, BLK), 1)
    causal = col_id <= row_id

    def attend(h):
        def body(i, carry):
            if h == 0:
                q = qa[pl.ds(2 * i, 2)].reshape(2 * BLK, 2 * BLK)
            else:
                q = jnp.concatenate(
                    [qa[pl.ds(2 * i, 2), :, BLK:], qb[pl.ds(2 * i, 2)]], axis=2
                ).reshape(2 * BLK, 2 * BLK)
            at = pl.ds(pl.multiple_of(i * 2 * BLK, BLK), KEYS)
            sc = lax.dot_general(q, kext[h, at, :], (((1,), (1,)), ((), ())),
                                 preferred_element_type=jnp.float32)
            halves = []
            for half in range(2):
                part = sc[half * BLK : (half + 1) * BLK]
                low = first_sm[2 * i + half] - (2 * i - (SEG_MOST - 1))
                tiles = []
                for u in range(half, half + SEG_MOST):
                    tile = part[:, u * BLK : (u + 1) * BLK]
                    ok = causal if u == half + SEG_MOST - 1 else (low <= u)
                    tiles.append(jnp.where(ok, tile, NEG))
                top = functools.reduce(jnp.maximum, tiles)
                top = jnp.max(top, axis=1, keepdims=True)
                w = [jnp.exp2((t - top) * EXP_SCALE).astype(jnp.bfloat16) for t in tiles]
                none = jnp.zeros((BLK, BLK), jnp.bfloat16)
                halves.append(jnp.concatenate(w + [none] if half == 0 else [none] + w, axis=1))
            o = jnp.dot(jnp.concatenate(halves, axis=0), vext[h, at, :],
                        preferred_element_type=jnp.float32)
            o = (o[:, :BLK] / o[:, BLK:]).astype(jnp.bfloat16)
            att[h, pl.ds(2 * i, 2)] = o.reshape(2, BLK, BLK)
            return carry

        lax.fori_loop(0, NBLK // 2, body, 0)

    def z_copy(h, d, slot):
        return remote(zsend.at[h, d], zrecv[h].at[slot], z_send.at[h, d], z_recv.at[h, d],
                      dp=(s + d) % N_DP)

    def send_dp(h):
        for d in list(range(1, N_DP)) + [0]:
            base = slot_sm[d]
            for j in range(SEG_MOST):
                tile = att[h, jnp.minimum(base + j, NBLK - 1)]
                if d == 0:
                    zrecv[h][s, j] = tile
                else:
                    zsend[h, d, j] = tile
            if d:
                z_copy(h, d, s).start()

    def o_copy(h, o, owner, peer):
        begin = pl.multiple_of((2 * owner + h) * BLK, BLK)
        return remote(osend.at[h, o], out.at[:, pl.ds(begin, BLK)], o_send.at[h, o], o_recv.at[h, o],
                      seq=peer)

    def o_own(h):
        begin = pl.multiple_of((2 * me + h) * BLK, BLK)
        return pltpu.make_async_copy(osend.at[h, 0], out.at[:, pl.ds(begin, BLK)], own_sem.at[2 + h])

    def send_seq(h):
        for d in range(1, N_DP):
            z_copy(h, d, (s + N_DP - d) % N_DP).wait_recv()

        def body(o, carry):
            peer = seq_peer(y, x, c, o)
            pick = pick_sm[peer]
            osend[h, o] = zrecv[h][pick // SEG_MOST, pick % SEG_MOST]
            o_copy(h, o, me, peer).start()
            return carry

        lax.fori_loop(1, N_SEQ, body, 0)
        pick = pick_sm[me]
        osend[h, 0] = zrecv[h][pick // SEG_MOST, pick % SEG_MOST]
        o_own(h).start()

    q_own(0).wait()
    q_own(1).wait()
    q_arrive(0)
    attend(0)
    send_dp(0)
    q_arrive(1)
    attend(1)
    send_dp(1)
    send_seq(0)
    send_seq(1)

    for cp in ph1 + ph2 + ph2b + sib:
        cp.wait_send()
    q_drain(0)
    q_drain(1)
    for h in range(2):
        for d in range(1, N_DP):
            z_copy(h, d, s).wait_send()
        o_own(h).wait()

        def body(o, carry):
            cp = o_copy(h, o, seq_source(y, x, c, o), seq_peer(y, x, c, o))
            cp.wait_send()
            cp.wait_recv()
            return carry

        lax.fori_loop(1, N_SEQ, body, 0)


def on_device(queries, kv_latent, key_rope, kv_gain, kv_up, segment_blocks, bucket_of, doc_breaks):
    bf16 = jnp.bfloat16
    rope2 = jnp.concatenate([key_rope, key_rope], axis=1)
    vmem = pl.BlockSpec(memory_space=pltpu.VMEM)
    smem = pl.BlockSpec(memory_space=pltpu.SMEM)
    anywhere = pl.BlockSpec(memory_space=pl.ANY)
    dma = pltpu.SemaphoreType.DMA
    return pl.pallas_call(
        kernel,
        out_shape=jax.ShapeDtypeStruct((BLK, N_SEQ * 2 * HD_V), bf16),
        in_specs=[anywhere, vmem, vmem, vmem, vmem, smem, smem, smem],
        out_specs=anywhere,
        scratch_shapes=[
            pltpu.VMEM((NY, NX, NC, 2, HALF, XW), bf16),
            pltpu.VMEM((NBLK, BLK, 2 * BLK), bf16),
            pltpu.VMEM((NBLK, BLK, BLK), bf16),
            pltpu.VMEM((LAT, 5 * BLK), bf16),
            pltpu.VMEM((2, LEAD + NBLK * BLK, 2 * BLK), bf16),
            pltpu.VMEM((2, LEAD + NBLK * BLK, 2 * BLK), bf16),
            pltpu.VMEM((2, NBLK, BLK, BLK), bf16),
            pltpu.VMEM((2, N_DP, SEG_MOST, BLK, BLK), bf16),
            pltpu.VMEM((N_DP, SEG_MOST, BLK, BLK), bf16),
            pltpu.VMEM((N_DP, SEG_MOST, BLK, BLK), bf16),
            pltpu.VMEM((2, N_SEQ, BLK, BLK), bf16),
            pltpu.SMEM((N_DP,), jnp.int32),
            pltpu.SMEM((NBLK,), jnp.int32),
            pltpu.SMEM((NBLK,), jnp.int32),
            pltpu.SMEM((N_DP,), jnp.int32),
            dma((2, 4)), dma((2, 4)), dma((2, 4)), dma((2, 4)), dma((2, 4)), dma((2, 4)),
            dma((2, N_SEQ)), dma((2, N_SEQ)),
            dma((2, N_DP)), dma((2, N_DP)),
            dma((2, N_SEQ)), dma((2, N_SEQ)),
            dma((4,)),
        ],
        compiler_params=pltpu.CompilerParams(
            collective_id=0, has_side_effects=True, vmem_limit_bytes=56 * 2**20
        ),
    )(queries, kv_latent, rope2, kv_gain.reshape(1, LAT), kv_up, segment_blocks, bucket_of, doc_breaks)


def solution(mesh):
    in_specs = (
        P(("dp", "seq"), None),
        P(("dp", "seq"), None),
        P(("dp", "seq"), None),
        P(),
        P(None, "seq"),
        P(),
        P(),
        P(),
    )
    return jax.shard_map(
        on_device, mesh=mesh, in_specs=in_specs, out_specs=P(("dp", "seq"), None), check_vma=False
    )
```

```python
import functools
import math

import jax
import jax.numpy as jnp
from jax import lax
from jax.experimental import pallas as pl
from jax.experimental.pallas import tpu as pltpu
from jax.sharding import PartitionSpec as P

HD_NOPE = 128
HD_ROPE = 64
HD_V = 128
BLK = 128
LAT = 512
NBLK = 32
N_DP = 8
SEG_MOST = 8
NY, NX, NC = 4, 4, 2
N_SEQ = NY * NX * NC
LEAD = (SEG_MOST - 1) * BLK
GROUP = 4
KEYS = LEAD + GROUP * BLK
XW = LAT + 2 * HD_ROPE
ROUNDS = 4
ORDER = (20, 21, 12, 24, 13, 25, 18, 6, 19, 7, 22, 2, 23, 3, 28, 8, 29, 9, 4, 16, 5, 17, 10, 30, 11, 31, 14, 26, 15, 27, 1)
Z_ORDER = (4, 3, 5, 2, 6, 1, 7, 0)
EPS = 1e-06
NEG = -1e30
EXP_SCALE = (HD_NOPE + HD_ROPE) ** -0.5 * math.log2(math.e)
HALF = BLK // 2


def seq_peer(y, x, c, o):
    dc, dx, dy = o % NC, (o // NC) % NX, o // (NC * NX)
    return ((y + dy) % NY) * (NX * NC) + ((x + dx) % NX) * NC + (c + dc) % NC


def seq_source(y, x, c, o):
    dc, dx, dy = o % NC, (o // NC) % NX, o // (NC * NX)
    return ((y + NY - dy) % NY) * (NX * NC) + ((x + NX - dx) % NX) * NC + (c + NC - dc) % NC


def kernel(
    queries, latent, rope2, gain, kv_up, seg, bucket_of, breaks,
    out,
    xall, qa, qb, wts, kext, vext, att, zsend, zrecv0, zrecv1, zrecv2, zrecv3, osend,
    starts_sm, first_sm, pick_sm, slot_sm,
    l1_send, l1_recv, l2_send, l2_recv, sib_send, sib_recv,
    q_send, q_recv, z_send, z_recv, o_send, o_recv, own_sem,
):
    s = lax.axis_index("dp")
    me = lax.axis_index("seq")
    y, x, c = me // (NX * NC), (me // NC) % NX, me % NC

    def remote(src, dst, send, recv, **axes):
        return pltpu.make_async_remote_copy(
            src_ref=src, dst_ref=dst, send_sem=send, recv_sem=recv,
            device_id=axes, device_id_type=pl.DeviceIdType.MESH,
        )

    zrecv = (zrecv0, zrecv1, zrecv2, zrecv3)

    barrier = pltpu.get_barrier_semaphore()

    def greet_seq(o, carry):
        pl.semaphore_signal(barrier, inc=1, device_id={"seq": seq_peer(y, x, c, o)},
                            device_id_type=pl.DeviceIdType.MESH)
        return carry

    lax.fori_loop(1, N_SEQ, greet_seq, 0)
    for d in range(1, N_DP):
        pl.semaphore_signal(barrier, inc=1, device_id={"dp": (s + d) % N_DP},
                            device_id_type=pl.DeviceIdType.MESH)

    lat = latent[...].astype(jnp.float32)
    normed = (
        lat * lax.rsqrt(jnp.mean(lat * lat, axis=1, keepdims=True) + EPS) * gain[...]
    ).astype(jnp.bfloat16)
    rows = jnp.concatenate([normed, rope2[...]], axis=1).reshape(2, HALF, XW)
    xall[y, x, c] = rows

    pl.semaphore_wait(barrier, N_SEQ - 1 + N_DP - 1)

    def at_x(d):
        return y * (NX * NC) + ((x + d) % NX) * NC + c

    def at_y(d):
        return ((y + d) % NY) * (NX * NC) + x * NC + c

    sibling = y * (NX * NC) + x * NC + (1 - c)
    ph1 = []
    for d in range(1, 4):
        own_a, own_b = xall.at[y, x, c, 0], xall.at[y, x, c, 1]
        ph1.append(remote(own_a, own_a, l1_send.at[0, d], l1_recv.at[0, d], seq=at_x(d)))
        ph1.append(remote(own_b, own_b, l1_send.at[1, d], l1_recv.at[1, d], seq=at_y(d)))
    for cp in ph1:
        cp.start()

    def q_copy(r, o, peer, slot):
        h, half = r // 2, r % 2
        width = BLK if h else 2 * BLK
        begin = pl.multiple_of(peer * (3 * BLK) + h * 2 * BLK, BLK)
        return remote(queries.at[pl.ds(half * HALF, HALF), pl.ds(begin, width)],
                      (qb if h else qa).at[half, slot], q_send.at[r, o], q_recv.at[r, o], seq=peer)

    def q_start(r):
        for o in ORDER:
            q_copy(r, o, seq_peer(y, x, c, o), me).start()

    def q_arrive(r):
        q_own(r).wait()

        def body(o, carry):
            q_copy(r, o, seq_peer(y, x, c, o), seq_source(y, x, c, o)).wait_recv()
            return carry
        lax.fori_loop(1, N_SEQ, body, 0)

    def q_drain(r):
        def body(o, carry):
            q_copy(r, o, seq_peer(y, x, c, o), me).wait_send()
            return carry
        lax.fori_loop(1, N_SEQ, body, 0)

    def q_own(r):
        h, half = r // 2, r % 2
        width = BLK if h else 2 * BLK
        begin = pl.multiple_of(me * (3 * BLK) + h * 2 * BLK, BLK)
        return pltpu.make_async_copy(queries.at[pl.ds(half * HALF, HALF), pl.ds(begin, width)],
                                     (qb if h else qa).at[half, me], own_sem.at[r])

    q_start(0)
    for r in range(ROUNDS):
        q_own(r).start()

    for d in range(1, 4):
        there = xall.at[y, (x + NX - d) % NX, c, 0]
        remote(there, there, l1_send.at[0, d], l1_recv.at[0, d], seq=at_x(d)).wait_recv()
    row_a = xall.at[y, :, c, 0]
    ph2 = [remote(row_a, row_a, l2_send.at[0, d], l2_recv.at[0, d], seq=at_y(d)) for d in range(1, 4)]
    for cp in ph2:
        cp.start()
    for d in range(1, 4):
        there = xall.at[(y + NY - d) % NY, x, c, 1]
        remote(there, there, l1_send.at[1, d], l1_recv.at[1, d], seq=at_y(d)).wait_recv()
    col_b = xall.at[:, x, c, 1]
    ph2b = [remote(col_b, col_b, l2_send.at[1, d], l2_recv.at[1, d], seq=at_x(d)) for d in range(1, 4)]
    for cp in ph2b:
        cp.start()
    sib = [
        remote(row_a, row_a, sib_send.at[0, 0], sib_recv.at[0, 0], seq=sibling),
        remote(col_b, col_b, sib_send.at[1, 0], sib_recv.at[1, 0], seq=sibling),
    ]
    for cp in sib:
        cp.start()

    q_start(1)

    total = jnp.int32(0)
    start_of = []
    for g in range(N_DP):
        start_of.append(total)
        starts_sm[g] = total
        total = total + seg[g]
    mine = jnp.int32(0)
    for j in range(N_DP):
        mine = mine + jnp.where(bucket_of[j] == s, j, 0)
    for d in range(N_DP):
        b = (s + d) % N_DP
        at = jnp.int32(0)
        for j in range(N_DP):
            at = at + jnp.where(bucket_of[j] == b, j, 0)
        slot_sm[d] = starts_sm[(at - s + N_DP) % N_DP]
    ends, begins = [], []
    total = jnp.int32(0)
    for r in range(N_DP):
        begins.append(total)
        total = total + seg[(mine - r + N_DP) % N_DP]
        ends.append(total)

    def plan_tile(k, first):
        begins_here = breaks[s, k] == 1
        pick = jnp.int32(0)
        for r in range(N_DP):
            begins_here = begins_here | (start_of[r] == k)
            inside = (k >= begins[r]) & (k < ends[r])
            pick = pick + jnp.where(inside, r * SEG_MOST + k - begins[r], 0)
        first = jnp.where(begins_here, k, first)
        first_sm[k] = first
        pick_sm[k] = pick
        return first

    lax.fori_loop(0, NBLK, plan_tile, jnp.int32(0))

    lane = lax.broadcasted_iota(jnp.int32, (LAT, BLK), 1)
    wts[:, : 2 * BLK] = kv_up[:, : 2 * BLK]
    turned = pltpu.roll(kv_up[:, 2 * BLK : 3 * BLK].astype(jnp.float32), HALF, 1)
    wts[:, 2 * BLK : 3 * BLK] = jnp.where(lane < HALF, 0.0, turned).astype(jnp.bfloat16)
    wts[:, 3 * BLK : 4 * BLK] = jnp.where(lane < HALF, turned, 0.0).astype(jnp.bfloat16)
    wts[:, 4 * BLK :] = kv_up[:, 3 * BLK :]
    kext[:, :LEAD, :] = jnp.zeros((2, LEAD, 2 * BLK), jnp.bfloat16)
    vext[:, :LEAD, :] = jnp.zeros((2, LEAD, 2 * BLK), jnp.bfloat16)

    for d in range(1, 4):
        got = xall.at[(y + NY - d) % NY, :, c, 0]
        remote(got, got, l2_send.at[0, d], l2_recv.at[0, d], seq=at_y(d)).wait_recv()
        sib.append(remote(got, got, sib_send.at[0, d], sib_recv.at[0, d], seq=sibling))
        sib[-1].start()
        got = xall.at[:, (x + NX - d) % NX, c, 1]
        remote(got, got, l2_send.at[1, d], l2_recv.at[1, d], seq=at_x(d)).wait_recv()
        sib.append(remote(got, got, sib_send.at[1, d], sib_recv.at[1, d], seq=sibling))
        sib[-1].start()
    for d in range(4):
        got = xall.at[(y + NY - d) % NY, :, 1 - c, 0]
        remote(got, got, sib_send.at[0, d], sib_recv.at[0, d], seq=sibling).wait_recv()
        got = xall.at[:, (x + NX - d) % NX, 1 - c, 1]
        remote(got, got, sib_send.at[1, d], sib_recv.at[1, d], seq=sibling).wait_recv()

    lane2 = lax.broadcasted_iota(jnp.int32, (2 * BLK, BLK), 1)

    def project(i, carry):
        block = xall[i // NX, i % NX].reshape(2 * BLK, XW)
        rot = block[:, LAT:].astype(jnp.float32)
        kv = jnp.dot(block[:, :LAT], wts[...], preferred_element_type=jnp.float32)
        at = pl.ds(pl.multiple_of(LEAD + i * 2 * BLK, BLK), 2 * BLK)
        ones = jnp.ones((2 * BLK, BLK), jnp.bfloat16)
        kext[0, at, :BLK] = kv[:, :BLK].astype(jnp.bfloat16)
        kext[0, at, BLK:] = jnp.where(lane2 < HALF, rot, 0.0).astype(jnp.bfloat16)
        vext[0, at, :BLK] = kv[:, BLK : 2 * BLK].astype(jnp.bfloat16)
        vext[0, at, BLK:] = ones
        kext[1, at, :BLK] = kv[:, 2 * BLK : 3 * BLK].astype(jnp.bfloat16)
        kext[1, at, BLK:] = jnp.where(lane2 < HALF, kv[:, 3 * BLK : 4 * BLK], rot).astype(jnp.bfloat16)
        vext[1, at, :BLK] = kv[:, 4 * BLK :].astype(jnp.bfloat16)
        vext[1, at, BLK:] = ones
        return carry

    lax.fori_loop(0, NBLK // 2, project, 0)
    q_start(2)
    q_start(3)

    row_id = lax.broadcasted_iota(jnp.int32, (HALF, BLK), 0)
    col_id = lax.broadcasted_iota(jnp.int32, (HALF, BLK), 1)
    none = jnp.zeros((HALF, BLK), jnp.bfloat16)

    def attend(r):
        h, half = r // 2, r % 2
        causal = col_id <= row_id + half * HALF

        def body(i, carry):
            of = pl.ds(GROUP * i, GROUP)
            if h == 0:
                q = qa[half, of]
            else:
                q = jnp.concatenate([qa[half, of, :, BLK:], qb[half, of]], axis=2)
            at = pl.ds(pl.multiple_of(i * GROUP * BLK, BLK), KEYS)
            sc = lax.dot_general(q.reshape(GROUP * HALF, 2 * BLK), kext[h, at, :],
                                 (((1,), (1,)), ((), ())), preferred_element_type=jnp.float32)
            parts = []
            for t in range(GROUP):
                part = sc[t * HALF : (t + 1) * HALF]
                low = first_sm[GROUP * i + t] - (GROUP * i - (SEG_MOST - 1))
                tiles = []
                for u in range(t, t + SEG_MOST):
                    tile = part[:, u * BLK : (u + 1) * BLK]
                    ok = causal if u == t + SEG_MOST - 1 else (low <= u)
                    tiles.append(jnp.where(ok, tile, NEG))
                top = functools.reduce(jnp.maximum, tiles)
                top = jnp.max(top, axis=1, keepdims=True)
                w = [jnp.exp2((e - top) * EXP_SCALE).astype(jnp.bfloat16) for e in tiles]
                parts.append(jnp.concatenate([none] * t + w + [none] * (GROUP - 1 - t), axis=1))
            o = jnp.dot(jnp.concatenate(parts, axis=0), vext[h, at, :],
                        preferred_element_type=jnp.float32)
            o = (o[:, :BLK] / o[:, BLK:]).astype(jnp.bfloat16)
            att[of] = o.reshape(GROUP, HALF, BLK)
            return carry

        lax.fori_loop(0, NBLK // GROUP, body, 0, unroll=2)

    def z_copy(r, d, slot):
        return remote(zsend.at[r, d], zrecv[r].at[slot], z_send.at[r, d], z_recv.at[r, d],
                      dp=(s + d) % N_DP)

    def send_dp(r):
        for d in Z_ORDER:
            base = slot_sm[d]
            for j in range(SEG_MOST):
                tile = att[jnp.minimum(base + j, NBLK - 1)]
                if d == 0:
                    zrecv[r][s, j] = tile
                else:
                    zsend[r, d, j] = tile
            if d:
                z_copy(r, d, s).start()

    def o_part(r, owner):
        begin = pl.multiple_of((2 * owner + r // 2) * BLK, BLK)
        return out.at[pl.ds(r % 2 * HALF, HALF), pl.ds(begin, BLK)]

    def o_copy(r, o, owner, peer):
        return remote(osend.at[r, o], o_part(r, owner), o_send.at[r, o], o_recv.at[r, o], seq=peer)

    def o_own(r):
        return pltpu.make_async_copy(osend.at[r, 0], o_part(r, me), own_sem.at[ROUNDS + r])

    def send_seq(r):
        for d in range(1, N_DP):
            z_copy(r, d, (s + N_DP - d) % N_DP).wait_recv()
        for o in ORDER:
            peer = seq_peer(y, x, c, o)
            pick = pick_sm[peer]
            osend[r, o] = zrecv[r][pick // SEG_MOST, pick % SEG_MOST]
            o_copy(r, o, me, peer).start()
        pick = pick_sm[me]
        osend[r, 0] = zrecv[r][pick // SEG_MOST, pick % SEG_MOST]
        o_own(r).start()

    for r in range(ROUNDS):
        q_arrive(r)
        attend(r)
        send_dp(r)
    for r in range(ROUNDS):
        send_seq(r)

    for cp in ph1 + ph2 + ph2b + sib:
        cp.wait_send()
    for r in range(ROUNDS):
        q_drain(r)
        for d in range(1, N_DP):
            z_copy(r, d, s).wait_send()
        o_own(r).wait()

        def body(o, carry):
            cp = o_copy(r, o, seq_source(y, x, c, o), seq_peer(y, x, c, o))
            cp.wait_send()
            cp.wait_recv()
            return carry

        lax.fori_loop(1, N_SEQ, body, 0)


def on_device(queries, kv_latent, key_rope, kv_gain, kv_up, segment_blocks, bucket_of, doc_breaks):
    bf16 = jnp.bfloat16
    rope2 = jnp.concatenate([key_rope, key_rope], axis=1)
    vmem = pl.BlockSpec(memory_space=pltpu.VMEM)
    smem = pl.BlockSpec(memory_space=pltpu.SMEM)
    anywhere = pl.BlockSpec(memory_space=pl.ANY)
    dma = pltpu.SemaphoreType.DMA
    return pl.pallas_call(
        kernel,
        out_shape=jax.ShapeDtypeStruct((BLK, N_SEQ * 2 * HD_V), bf16),
        in_specs=[anywhere, vmem, vmem, vmem, vmem, smem, smem, smem],
        out_specs=anywhere,
        scratch_shapes=[
            pltpu.VMEM((NY, NX, NC, 2, HALF, XW), bf16),
            pltpu.VMEM((2, NBLK, HALF, 2 * BLK), bf16),
            pltpu.VMEM((2, NBLK, HALF, BLK), bf16),
            pltpu.VMEM((LAT, 5 * BLK), bf16),
            pltpu.VMEM((2, LEAD + NBLK * BLK, 2 * BLK), bf16),
            pltpu.VMEM((2, LEAD + NBLK * BLK, 2 * BLK), bf16),
            pltpu.VMEM((NBLK, HALF, BLK), bf16),
            pltpu.VMEM((ROUNDS, N_DP, SEG_MOST, HALF, BLK), bf16),
            *[pltpu.VMEM((N_DP, SEG_MOST, HALF, BLK), bf16)] * ROUNDS,
            pltpu.VMEM((ROUNDS, N_SEQ, HALF, BLK), bf16),
            pltpu.SMEM((N_DP,), jnp.int32),
            pltpu.SMEM((NBLK,), jnp.int32),
            pltpu.SMEM((NBLK,), jnp.int32),
            pltpu.SMEM((N_DP,), jnp.int32),
            dma((2, 4)), dma((2, 4)), dma((2, 4)), dma((2, 4)), dma((2, 4)), dma((2, 4)),
            dma((ROUNDS, N_SEQ)), dma((ROUNDS, N_SEQ)),
            dma((ROUNDS, N_DP)), dma((ROUNDS, N_DP)),
            dma((ROUNDS, N_SEQ)), dma((ROUNDS, N_SEQ)),
            dma((2 * ROUNDS,)),
        ],
        compiler_params=pltpu.CompilerParams(
            collective_id=0, has_side_effects=True, vmem_limit_bytes=56 * 2**20
        ),
    )(queries, kv_latent, rope2, kv_gain.reshape(1, LAT), kv_up, segment_blocks, bucket_of, doc_breaks)


def solution(mesh):
    in_specs = (
        P(("dp", "seq"), None),
        P(("dp", "seq"), None),
        P(("dp", "seq"), None),
        P(),
        P(None, "seq"),
        P(),
        P(),
        P(),
    )
    return jax.shard_map(
        on_device, mesh=mesh, in_specs=in_specs, out_specs=P(("dp", "seq"), None), check_vma=False
    )
```

```python
import functools
import math

import jax
import jax.numpy as jnp
from jax import lax
from jax.experimental import pallas as pl
from jax.experimental.pallas import tpu as pltpu
from jax.sharding import PartitionSpec as P

HD_NOPE = 128
HD_ROPE = 64
HD_V = 128
BLK = 128
HALF = BLK // 2
LAT = 512
NBLK = 32
N_DP = 8
SEG_MOST = 8
NY, NX, NC = 4, 4, 2
N_SEQ = NY * NX * NC
LEAD = (SEG_MOST - 1) * BLK
GROUP = 4
KEYS = LEAD + GROUP * BLK
XW = LAT + 2 * HD_ROPE
ROUNDS = 4
ORDER = (20, 21, 12, 24, 13, 25, 18, 6, 19, 7, 22, 2, 23, 3, 28, 8, 29, 9, 4, 16, 5, 17, 10, 30, 11, 31, 14, 26, 15, 27, 1)
Z_ORDER = (4, 3, 5, 2, 6, 1, 7, 0)
EARLY = 10
DIRECT = 4
RELAYED = 12
PIECE = HALF + (RELAYED - N_DP) * HALF // N_DP
EPS = 1e-06
NEG = -1e30
EXP_SCALE = (HD_NOPE + HD_ROPE) ** -0.5 * math.log2(math.e)


def seq_peer(y, x, c, o):
    dc, dx, dy = o % NC, (o // NC) % NX, o // (NC * NX)
    return ((y + dy) % NY) * (NX * NC) + ((x + dx) % NX) * NC + (c + dc) % NC


def seq_source(y, x, c, o):
    dc, dx, dy = o % NC, (o // NC) % NX, o // (NC * NX)
    return ((y + NY - dy) % NY) * (NX * NC) + ((x + NX - dx) % NX) * NC + (c + NC - dc) % NC


def kernel(
    queries, latent, rope2, gain, kv_up, seg, bucket_of, breaks,
    out,
    xa0, xa1, xa2, xa3, xb0, xb1, xb2, xb3, qa, qb, wts, kext, vext, att, zsend, zrecv0, zrecv1, zrecv2, zrecv3, rsend, rrecv0, rrecv1, rrecv2, rrecv3, fsend, osend,
    starts_sm, first_sm, pick_sm, slot_sm, over_sm, tile_sm, seg_sm, inv_sm,
    l1_send, l1_recv, l2_send, l2_recv, sib_send, sib_recv,
    q_send, q_recv, z_send, z_recv, r_send, r_recv, f_send, f_recv, o_send, o_recv, own_sem,
):
    s = lax.axis_index("dp")
    me = lax.axis_index("seq")
    y, x, c = me // (NX * NC), (me // NC) % NX, me % NC

    def remote(src, dst, send, recv, **axes):
        return pltpu.make_async_remote_copy(
            src_ref=src, dst_ref=dst, send_sem=send, recv_sem=recv,
            device_id=axes, device_id_type=pl.DeviceIdType.MESH,
        )

    xa, xb = (xa0, xa1, xa2, xa3), (xb0, xb1, xb2, xb3)
    zrecv = (zrecv0, zrecv1, zrecv2, zrecv3)
    rrecv = (rrecv0, rrecv1, rrecv2, rrecv3)

    barrier = pltpu.get_barrier_semaphore()

    def greet_seq(o, carry):
        pl.semaphore_signal(barrier, inc=1, device_id={"seq": seq_peer(y, x, c, o)},
                            device_id_type=pl.DeviceIdType.MESH)
        return carry

    lax.fori_loop(1, N_SEQ, greet_seq, 0)
    for d in range(1, N_DP):
        pl.semaphore_signal(barrier, inc=1, device_id={"dp": (s + d) % N_DP},
                            device_id_type=pl.DeviceIdType.MESH)

    lat = latent[...].astype(jnp.float32)
    normed = (
        lat * lax.rsqrt(jnp.mean(lat * lat, axis=1, keepdims=True) + EPS) * gain[...]
    ).astype(jnp.bfloat16)
    rows = jnp.concatenate([normed, rope2[...]], axis=1)
    xa0[x, c] = rows[:HALF]
    xb0[y, c] = rows[HALF:]

    pl.semaphore_wait(barrier, N_SEQ - 1 + N_DP - 1)

    def at_x(d):
        return y * (NX * NC) + ((x + d) % NX) * NC + c

    def at_y(d):
        return ((y + d) % NY) * (NX * NC) + x * NC + c

    sibling = y * (NX * NC) + x * NC + (1 - c)
    ph1 = []
    for d in range(1, 4):
        own_a, own_b = xa0.at[x, c], xb0.at[y, c]
        ph1.append(remote(own_a, own_a, l1_send.at[0, d], l1_recv.at[0, d], seq=at_x(d)))
        ph1.append(remote(own_b, own_b, l1_send.at[1, d], l1_recv.at[1, d], seq=at_y(d)))
    for cp in ph1:
        cp.start()

    def q_copy(r, o, peer, slot):
        h, half = r // 2, r % 2
        width = BLK if h else 2 * BLK
        begin = pl.multiple_of(peer * (3 * BLK) + h * 2 * BLK, BLK)
        return remote(queries.at[pl.ds(half * HALF, HALF), pl.ds(begin, width)],
                      (qb if h else qa).at[half, slot], q_send.at[r, o], q_recv.at[r, o], seq=peer)

    def q_start(r, order=ORDER):
        for o in order:
            q_copy(r, o, seq_peer(y, x, c, o), me).start()

    def q_arrive(r):
        q_own(r).wait()

        def body(o, carry):
            q_copy(r, o, seq_peer(y, x, c, o), seq_source(y, x, c, o)).wait_recv()
            return carry
        lax.fori_loop(1, N_SEQ, body, 0)

    def q_drain(r):
        def body(o, carry):
            q_copy(r, o, seq_peer(y, x, c, o), me).wait_send()
            return carry
        lax.fori_loop(1, N_SEQ, body, 0)

    def q_own(r):
        h, half = r // 2, r % 2
        width = BLK if h else 2 * BLK
        begin = pl.multiple_of(me * (3 * BLK) + h * 2 * BLK, BLK)
        return pltpu.make_async_copy(queries.at[pl.ds(half * HALF, HALF), pl.ds(begin, width)],
                                     (qb if h else qa).at[half, me], own_sem.at[r])

    q_start(0, ORDER[:EARLY])
    for r in range(ROUNDS):
        q_own(r).start()

    for d in range(1, 4):
        there = xa0.at[(x + NX - d) % NX, c]
        remote(there, there, l1_send.at[0, d], l1_recv.at[0, d], seq=at_x(d)).wait_recv()
    row_a = xa0.at[:, c]
    ph2 = [remote(row_a, xa[d].at[:, c], l2_send.at[0, d], l2_recv.at[0, d], seq=at_y(d)) for d in range(1, 4)]
    for cp in ph2:
        cp.start()
    for d in range(1, 4):
        there = xb0.at[(y + NY - d) % NY, c]
        remote(there, there, l1_send.at[1, d], l1_recv.at[1, d], seq=at_y(d)).wait_recv()
    col_b = xb0.at[:, c]
    ph2b = [remote(col_b, xb[d].at[:, c], l2_send.at[1, d], l2_recv.at[1, d], seq=at_x(d)) for d in range(1, 4)]
    for cp in ph2b:
        cp.start()
    sib = [
        remote(row_a, row_a, sib_send.at[0, 0], sib_recv.at[0, 0], seq=sibling),
        remote(col_b, col_b, sib_send.at[1, 0], sib_recv.at[1, 0], seq=sibling),
    ]
    for cp in sib:
        cp.start()

    q_start(0, ORDER[EARLY:])

    total, over = jnp.int32(0), jnp.int32(0)
    start_of, over_of = [], []
    for g in range(N_DP):
        start_of.append(total)
        starts_sm[g] = total
        total = total + seg[g]
        over_of.append(over)
        over_sm[g] = over
        over = over + jnp.maximum(seg[g] - DIRECT, 0)
    over_of.append(over)
    mine = jnp.int32(0)
    for d in range(N_DP):
        b = (s + d) % N_DP
        at = jnp.int32(0)
        for j in range(N_DP):
            at = at + jnp.where(bucket_of[j] == b, j, 0)
        if d == 0:
            mine = at
        inv_sm[d] = at
        slot_sm[d] = starts_sm[(at - s + N_DP) % N_DP]

    def plan_over(k, carry):
        tile, of = jnp.int32(0), jnp.int32(0)
        for g in range(N_DP):
            inside = (k >= over_of[g]) & (k < over_of[g + 1])
            tile = tile + jnp.where(inside, start_of[g] + DIRECT + k - over_of[g], 0)
            of = of + jnp.where(inside, g, 0)
        tile_sm[k] = tile
        seg_sm[k] = of
        return carry

    lax.fori_loop(0, RELAYED, plan_over, 0)
    ends, begins, overs = [], [], []
    total = jnp.int32(0)
    for r in range(N_DP):
        begins.append(total)
        overs.append(over_sm[(mine - r + N_DP) % N_DP])
        total = total + seg[(mine - r + N_DP) % N_DP]
        ends.append(total)

    def plan_tile(k, first):
        begins_here = breaks[s, k] == 1
        pick = jnp.int32(0)
        for r in range(N_DP):
            begins_here = begins_here | (start_of[r] == k)
            inside = (k >= begins[r]) & (k < ends[r])
            within = k - begins[r]
            place = jnp.where(within < DIRECT, r * DIRECT + within,
                              N_DP * DIRECT + overs[r] + within - DIRECT)
            pick = pick + jnp.where(inside, place, 0)
        first = jnp.where(begins_here, k, first)
        first_sm[k] = first
        pick_sm[k] = pick
        return first

    lax.fori_loop(0, NBLK, plan_tile, jnp.int32(0))

    lane = lax.broadcasted_iota(jnp.int32, (LAT, BLK), 1)
    wts[:, : 2 * BLK] = kv_up[:, : 2 * BLK]
    turned = pltpu.roll(kv_up[:, 2 * BLK : 3 * BLK].astype(jnp.float32), HALF, 1)
    wts[:, 2 * BLK : 3 * BLK] = jnp.where(lane < HALF, 0.0, turned).astype(jnp.bfloat16)
    wts[:, 3 * BLK : 4 * BLK] = jnp.where(lane < HALF, turned, 0.0).astype(jnp.bfloat16)
    wts[:, 4 * BLK :] = kv_up[:, 3 * BLK :]
    kext[:, :LEAD, :] = jnp.zeros((2, LEAD, 2 * BLK), jnp.bfloat16)
    vext[:, :LEAD, :BLK] = jnp.zeros((2, LEAD, BLK), jnp.bfloat16)
    vext[:, :, BLK:] = jnp.ones((2, LEAD + NBLK * BLK, BLK), jnp.bfloat16)

    lane4 = lax.broadcasted_iota(jnp.int32, (NX * NC * HALF, BLK), 1)

    def project(half, held, chips):
        block = held[...].reshape(NX * NC * HALF, XW)
        rot = block[:, LAT:].astype(jnp.float32)
        kv = jnp.dot(block[:, :LAT], wts[...], preferred_element_type=jnp.float32)
        k0 = kv[:, :BLK].astype(jnp.bfloat16)
        r0 = jnp.where(lane4 < HALF, rot, 0.0).astype(jnp.bfloat16)
        v0 = kv[:, BLK : 2 * BLK].astype(jnp.bfloat16)
        k1 = kv[:, 2 * BLK : 3 * BLK].astype(jnp.bfloat16)
        r1 = jnp.where(lane4 < HALF, kv[:, 3 * BLK : 4 * BLK], rot).astype(jnp.bfloat16)
        v1 = kv[:, 4 * BLK :].astype(jnp.bfloat16)
        for p in range(NX):
            for q in range(NC):
                chip = chips * NX + p if half == 0 else p * NX + chips
                begin = LEAD + (chip * NC + q) * BLK + half * HALF
                at = pl.ds(pl.multiple_of(begin, HALF), HALF)
                of = slice((p * NC + q) * HALF, (p * NC + q + 1) * HALF)
                kext[0, at, :BLK] = k0[of]
                kext[0, at, BLK:] = r0[of]
                vext[0, at, :BLK] = v0[of]
                kext[1, at, :BLK] = k1[of]
                kext[1, at, BLK:] = r1[of]
                vext[1, at, :BLK] = v1[of]

    def pass_on(d):
        got = xa[d].at[:, c]
        remote(got, got, l2_send.at[0, d], l2_recv.at[0, d], seq=at_y(d)).wait_recv()
        sib.append(remote(got, got, sib_send.at[0, d], sib_recv.at[0, d], seq=sibling))
        sib[-1].start()
        got = xb[d].at[:, c]
        remote(got, got, l2_send.at[1, d], l2_recv.at[1, d], seq=at_x(d)).wait_recv()
        sib.append(remote(got, got, sib_send.at[1, d], sib_recv.at[1, d], seq=sibling))
        sib[-1].start()

    def take_in(d):
        got = xa[d].at[:, 1 - c]
        remote(got, got, sib_send.at[0, d], sib_recv.at[0, d], seq=sibling).wait_recv()
        project(0, xa[d], (y + NY - d) % NY)
        got = xb[d].at[:, 1 - c]
        remote(got, got, sib_send.at[1, d], sib_recv.at[1, d], seq=sibling).wait_recv()
        project(1, xb[d], (x + NX - d) % NX)

    take_in(0)
    pass_on(1)
    pass_on(3)
    take_in(1)
    pass_on(2)
    q_start(1)
    take_in(3)
    take_in(2)
    q_start(2)
    q_start(3)

    row_id = lax.broadcasted_iota(jnp.int32, (HALF, BLK), 0)
    col_id = lax.broadcasted_iota(jnp.int32, (HALF, BLK), 1)
    none = jnp.zeros((HALF, BLK), jnp.bfloat16)

    def attend(r):
        h, half = r // 2, r % 2
        causal = col_id <= row_id + half * HALF

        def body(i, carry):
            of = pl.ds(GROUP * i, GROUP)
            if h == 0:
                q = qa[half, of]
            else:
                q = jnp.concatenate([qa[half, of, :, BLK:], qb[half, of]], axis=2)
            at = pl.ds(pl.multiple_of(i * GROUP * BLK, BLK), KEYS)
            sc = lax.dot_general(q.reshape(GROUP * HALF, 2 * BLK), kext[h, at, :],
                                 (((1,), (1,)), ((), ())), preferred_element_type=jnp.float32)
            parts = []
            for t in range(GROUP):
                part = sc[t * HALF : (t + 1) * HALF]
                low = first_sm[GROUP * i + t] - (GROUP * i - (SEG_MOST - 1))
                tiles = []
                for u in range(t, t + SEG_MOST):
                    tile = part[:, u * BLK : (u + 1) * BLK]
                    ok = causal if u == t + SEG_MOST - 1 else (low <= u)
                    tiles.append(jnp.where(ok, tile, NEG))
                top = functools.reduce(jnp.maximum, tiles)
                top = jnp.max(top, axis=1, keepdims=True)
                w = [jnp.exp2((e - top) * EXP_SCALE).astype(jnp.bfloat16) for e in tiles]
                parts.append(jnp.concatenate([none] * t + w + [none] * (GROUP - 1 - t), axis=1))
            o = jnp.dot(jnp.concatenate(parts, axis=0), vext[h, at, :],
                        preferred_element_type=jnp.float32)
            o = (o[:, :BLK] / o[:, BLK:]).astype(jnp.bfloat16)
            att[of] = o.reshape(GROUP, HALF, BLK)
            return carry

        lax.fori_loop(0, NBLK // GROUP, body, 0, unroll=2)

    rest = PIECE - HALF

    def z_copy(r, d, source):
        return remote(zsend.at[r, d], zrecv[r].at[pl.ds(source * DIRECT, DIRECT)],
                      z_send.at[r, d], z_recv.at[r, d], dp=(s + d) % N_DP)

    def r_copy(r, d, source):
        return remote(rsend.at[r, d], rrecv[r].at[source], r_send.at[r, d], r_recv.at[r, d],
                      dp=(s + d) % N_DP)

    def f_places(r, relay):
        places = [zrecv[r].at[N_DP * DIRECT + relay]]
        if rest:
            part = pl.ds(pl.multiple_of(relay % 2 * rest, rest), rest)
            places.append(zrecv[r].at[N_DP * DIRECT + N_DP + relay // 2, part])
        return places

    def f_copies(r, d, relay):
        places = f_places(r, relay)
        pieces = [fsend.at[r, d, pl.ds(0, HALF)]]
        if rest:
            pieces.append(fsend.at[r, d, pl.ds(HALF, rest)])
        return [remote(a, b, f_send.at[r, e, d], f_recv.at[r, e, d], dp=(s + d) % N_DP)
                for e, (a, b) in enumerate(zip(pieces, places))]

    def send_relays(r):
        for d in Z_ORDER:
            relay = (s + d) % N_DP
            dst = rrecv[r].at[s] if d == 0 else rsend.at[r, d]
            dst[:HALF] = att[tile_sm[relay]]
            if rest:
                part = pl.ds(pl.multiple_of(relay % 2 * rest, rest), rest)
                dst[HALF:] = att[tile_sm[N_DP + relay // 2], part]
            if d:
                r_copy(r, d, s).start()

    def send_dp(r):
        for d in Z_ORDER:
            base = slot_sm[d]
            for j in range(DIRECT):
                tile = att[jnp.minimum(base + j, NBLK - 1)]
                if d == 0:
                    zrecv[r][s * DIRECT + j] = tile
                else:
                    zsend[r, d, j] = tile
            if d:
                z_copy(r, d, s).start()

    def forward(r):
        for d in range(1, N_DP):
            r_copy(r, d, (s + N_DP - d) % N_DP).wait_recv()
        for d in Z_ORDER:
            source = (inv_sm[d] - seg_sm[s] + N_DP) % N_DP
            tile = rrecv[r][source, :HALF]
            if rest:
                source = (inv_sm[d] - seg_sm[N_DP + s // 2] + N_DP) % N_DP
                more = rrecv[r][source, HALF:]
            if d:
                fsend[r, d, :HALF] = tile
                if rest:
                    fsend[r, d, HALF:] = more
                for cp in f_copies(r, d, s):
                    cp.start()
            else:
                places = f_places(r, s)
                places[0][...] = tile
                if rest:
                    places[1][...] = more

    def o_part(r, owner):
        begin = pl.multiple_of((2 * owner + r // 2) * BLK, BLK)
        return out.at[pl.ds(r % 2 * HALF, HALF), pl.ds(begin, BLK)]

    def o_copy(r, o, owner, peer):
        return remote(osend.at[r, o], o_part(r, owner), o_send.at[r, o], o_recv.at[r, o], seq=peer)

    def o_own(r):
        return pltpu.make_async_copy(osend.at[r, 0], o_part(r, me), own_sem.at[ROUNDS + r])

    def send_seq(r):
        for d in range(1, N_DP):
            z_copy(r, d, (s + N_DP - d) % N_DP).wait_recv()
            for cp in f_copies(r, d, (s + N_DP - d) % N_DP):
                cp.wait_recv()
        for o in ORDER:
            peer = seq_peer(y, x, c, o)
            osend[r, o] = zrecv[r][pick_sm[peer]]
            o_copy(r, o, me, peer).start()
        osend[r, 0] = zrecv[r][pick_sm[me]]
        o_own(r).start()

    for r in range(ROUNDS):
        q_arrive(r)
        attend(r)
        if r:
            forward(r - 1)
        send_relays(r)
        send_dp(r)
    send_seq(0)
    forward(ROUNDS - 1)
    for r in range(1, ROUNDS):
        send_seq(r)

    for cp in ph1 + ph2 + ph2b + sib:
        cp.wait_send()
    for r in range(ROUNDS):
        q_drain(r)
        for d in range(1, N_DP):
            for cp in [z_copy(r, d, s), r_copy(r, d, s)] + f_copies(r, d, s):
                cp.wait_send()
        o_own(r).wait()

        def body(o, carry):
            cp = o_copy(r, o, seq_source(y, x, c, o), seq_peer(y, x, c, o))
            cp.wait_send()
            cp.wait_recv()
            return carry

        lax.fori_loop(1, N_SEQ, body, 0)


def on_device(queries, kv_latent, key_rope, kv_gain, kv_up, segment_blocks, bucket_of, doc_breaks):
    bf16 = jnp.bfloat16
    rope2 = jnp.concatenate([key_rope, key_rope], axis=1)
    vmem = pl.BlockSpec(memory_space=pltpu.VMEM)
    smem = pl.BlockSpec(memory_space=pltpu.SMEM)
    anywhere = pl.BlockSpec(memory_space=pl.ANY)
    dma = pltpu.SemaphoreType.DMA
    return pl.pallas_call(
        kernel,
        out_shape=jax.ShapeDtypeStruct((BLK, N_SEQ * 2 * HD_V), bf16),
        in_specs=[anywhere, vmem, vmem, vmem, vmem, smem, smem, smem],
        out_specs=anywhere,
        scratch_shapes=[
            *[pltpu.VMEM((NX, NC, HALF, XW), bf16)] * 8,
            pltpu.VMEM((2, NBLK, HALF, 2 * BLK), bf16),
            pltpu.VMEM((2, NBLK, HALF, BLK), bf16),
            pltpu.VMEM((LAT, 5 * BLK), bf16),
            pltpu.VMEM((2, LEAD + NBLK * BLK, 2 * BLK), bf16),
            pltpu.VMEM((2, LEAD + NBLK * BLK, 2 * BLK), bf16),
            pltpu.VMEM((NBLK, HALF, BLK), bf16),
            pltpu.VMEM((ROUNDS, N_DP, DIRECT, HALF, BLK), bf16),
            *[pltpu.VMEM((N_DP * DIRECT + RELAYED, HALF, BLK), bf16)] * ROUNDS,
            pltpu.VMEM((ROUNDS, N_DP, PIECE, BLK), bf16),
            *[pltpu.VMEM((N_DP, PIECE, BLK), bf16)] * ROUNDS,
            pltpu.VMEM((ROUNDS, N_DP, PIECE, BLK), bf16),
            pltpu.VMEM((ROUNDS, N_SEQ, HALF, BLK), bf16),
            *[pltpu.SMEM((n,), jnp.int32)
              for n in (N_DP, NBLK, NBLK, N_DP, N_DP, RELAYED, RELAYED, N_DP)],
            dma((2, 4)), dma((2, 4)), dma((2, 4)), dma((2, 4)), dma((2, 4)), dma((2, 4)),
            dma((ROUNDS, N_SEQ)), dma((ROUNDS, N_SEQ)),
            dma((ROUNDS, N_DP)), dma((ROUNDS, N_DP)),
            dma((ROUNDS, N_DP)), dma((ROUNDS, N_DP)),
            dma((ROUNDS, 2, N_DP)), dma((ROUNDS, 2, N_DP)),
            dma((ROUNDS, N_SEQ)), dma((ROUNDS, N_SEQ)),
            dma((2 * ROUNDS,)),
        ],
        compiler_params=pltpu.CompilerParams(
            collective_id=0, has_side_effects=True, vmem_limit_bytes=56 * 2**20
        ),
    )(queries, kv_latent, rope2, kv_gain.reshape(1, LAT), kv_up, segment_blocks, bucket_of, doc_breaks)


def solution(mesh):
    in_specs = (
        P(("dp", "seq"), None),
        P(("dp", "seq"), None),
        P(("dp", "seq"), None),
        P(),
        P(None, "seq"),
        P(),
        P(),
        P(),
    )
    return jax.shard_map(
        on_device, mesh=mesh, in_specs=in_specs, out_specs=P(("dp", "seq"), None), check_vma=False
    )
```

```python
import functools
import math

import jax
import jax.numpy as jnp
from jax import lax
from jax.experimental import pallas as pl
from jax.experimental.pallas import tpu as pltpu
from jax.sharding import PartitionSpec as P

HD_NOPE = 128
HD_ROPE = 64
HD_V = 128
BLK = 128
HALF = BLK // 2
LAT = 512
NBLK = 32
N_DP = 8
SEG_MOST = 8
NY, NX, NC = 4, 4, 2
N_SEQ = NY * NX * NC
LEAD = (SEG_MOST - 1) * BLK
GROUP = 4
KEYS = LEAD + GROUP * BLK
XW = LAT + 2 * HD_ROPE
ROUNDS = 4
ORDER = (20, 21, 12, 24, 13, 25, 18, 6, 19, 7, 22, 2, 23, 3, 28, 8, 29, 9, 4, 16, 5, 17, 10, 30, 11, 31, 14, 26, 15, 27, 1)
Z_ORDER = (4, 3, 5, 2, 6, 1, 7, 0)
EARLY = 10
NEAR = (1, 3, 2)
DIRECT = 4
RELAYS = (8, 12)
EPS = 1e-06
NEG = -1e30
EXP_SCALE = (HD_NOPE + HD_ROPE) ** -0.5 * math.log2(math.e)


def seq_peer(y, x, c, o):
    dc, dx, dy = o % NC, (o // NC) % NX, o // (NC * NX)
    return ((y + dy) % NY) * (NX * NC) + ((x + dx) % NX) * NC + (c + dc) % NC


def seq_source(y, x, c, o):
    dc, dx, dy = o % NC, (o // NC) % NX, o // (NC * NX)
    return ((y + NY - dy) % NY) * (NX * NC) + ((x + NX - dx) % NX) * NC + (c + NC - dc) % NC


def kernel(
    relayed,
    queries, latent, rope_t, gain, kv_up, seg, bucket_of, breaks,
    out,
    xa0, xa1, xa2, xa3, xb0, xb1, xb2, xb3, qa, qb, wts, kext, vext, att, zsend, zrecv0, zrecv1, zrecv2, zrecv3, rsend, rrecv0, rrecv1, rrecv2, rrecv3, fsend, osend,
    starts_sm, first_sm, pick_sm, slot_sm, over_sm, tile_sm, seg_sm, inv_sm,
    l1_send, l1_recv, l2_send, l2_recv, sib_send, sib_recv,
    q_send, q_recv, z_send, z_recv, r_send, r_recv, f_send, f_recv, o_send, o_recv, own_sem,
):
    s = lax.axis_index("dp")
    me = lax.axis_index("seq")
    y, x, c = me // (NX * NC), (me // NC) % NX, me % NC

    def remote(src, dst, send, recv, **axes):
        return pltpu.make_async_remote_copy(
            src_ref=src, dst_ref=dst, send_sem=send, recv_sem=recv,
            device_id=axes, device_id_type=pl.DeviceIdType.MESH,
        )

    xa, xb = (xa0, xa1, xa2, xa3), (xb0, xb1, xb2, xb3)
    zrecv = (zrecv0, zrecv1, zrecv2, zrecv3)
    rrecv = (rrecv0, rrecv1, rrecv2, rrecv3)

    barrier = pltpu.get_barrier_semaphore()

    def greet_seq(o, carry):
        pl.semaphore_signal(barrier, inc=1, device_id={"seq": seq_peer(y, x, c, o)},
                            device_id_type=pl.DeviceIdType.MESH)
        return carry

    lax.fori_loop(1, N_SEQ, greet_seq, 0)
    for d in range(1, N_DP):
        pl.semaphore_signal(barrier, inc=1, device_id={"dp": (s + d) % N_DP},
                            device_id_type=pl.DeviceIdType.MESH)

    lat = latent[...].astype(jnp.float32)
    normed = (
        lat * lax.rsqrt(jnp.mean(lat * lat, axis=1, keepdims=True) + EPS) * gain[...]
    ).astype(jnp.bfloat16)
    rope = rope_t[...].astype(jnp.float32)
    rope2 = jnp.transpose(jnp.concatenate([rope, rope], axis=0)).astype(jnp.bfloat16)
    rows = jnp.concatenate([normed, rope2], axis=1)
    xa0[x, c] = rows[:HALF]
    xb0[y, c] = rows[HALF:]

    pl.semaphore_wait(barrier, N_SEQ - 1 + N_DP - 1)

    def at_x(d):
        return y * (NX * NC) + ((x + d) % NX) * NC + c

    def at_y(d):
        return ((y + d) % NY) * (NX * NC) + x * NC + c

    sibling = y * (NX * NC) + x * NC + (1 - c)
    def ph1_copy(half, d, place):
        ref = xa0.at[place, c] if half == 0 else xb0.at[place, c]
        return remote(ref, ref, l1_send.at[half, d], l1_recv.at[half, d], seq=at_x(d) if half == 0 else at_y(d))

    def ph2_copy(half, d, p):
        if half == 0:
            place = (x + NX - p) % NX
            src, dst, peer = xa0.at[place, c], xa[d].at[place, c], at_y(d)
        else:
            place = (y + NY - p) % NY
            src, dst, peer = xb0.at[place, c], xb[d].at[place, c], at_x(d)
        return remote(src, dst, l2_send.at[half, d, p], l2_recv.at[half, d, p], seq=peer)

    def sib_copy(half, d):
        ref = (xa if half == 0 else xb)[d].at[:, c]
        return remote(ref, ref, sib_send.at[half, d], sib_recv.at[half, d], seq=sibling)

    for d in NEAR:
        ph1_copy(0, d, x).start()
        ph1_copy(1, d, y).start()
    for d in NEAR:
        ph2_copy(0, d, 0).start()
        ph2_copy(1, d, 0).start()

    def q_copy(r, o, peer, slot):
        h, half = r // 2, r % 2
        width = BLK if h else 2 * BLK
        begin = pl.multiple_of(peer * (3 * BLK) + h * 2 * BLK, BLK)
        return remote(queries.at[pl.ds(half * HALF, HALF), pl.ds(begin, width)],
                      (qb if h else qa).at[half, slot], q_send.at[r, o], q_recv.at[r, o], seq=peer)

    def q_start(r, order=ORDER):
        for o in order:
            q_copy(r, o, seq_peer(y, x, c, o), me).start()

    def q_arrive(r):
        q_own(r).wait()

        def body(o, carry):
            q_copy(r, o, seq_peer(y, x, c, o), seq_source(y, x, c, o)).wait_recv()
            return carry
        lax.fori_loop(1, N_SEQ, body, 0)

    def q_drain(r):
        def body(o, carry):
            q_copy(r, o, seq_peer(y, x, c, o), me).wait_send()
            return carry
        lax.fori_loop(1, N_SEQ, body, 0)

    def q_own(r):
        h, half = r // 2, r % 2
        width = BLK if h else 2 * BLK
        begin = pl.multiple_of(me * (3 * BLK) + h * 2 * BLK, BLK)
        return pltpu.make_async_copy(queries.at[pl.ds(half * HALF, HALF), pl.ds(begin, width)],
                                     (qb if h else qa).at[half, me], own_sem.at[r])

    q_start(0, ORDER[:EARLY])
    for r in range(ROUNDS):
        q_own(r).start()

    for p in NEAR:
        ph1_copy(0, p, (x + NX - p) % NX).wait_recv()
        for d in NEAR:
            ph2_copy(0, d, p).start()
        ph1_copy(1, p, (y + NY - p) % NY).wait_recv()
        for d in NEAR:
            ph2_copy(1, d, p).start()
    for half in range(2):
        sib_copy(half, 0).start()

    q_start(0, ORDER[EARLY:])

    total, over = jnp.int32(0), jnp.int32(0)
    start_of, over_of = [], []
    for g in range(N_DP):
        start_of.append(total)
        starts_sm[g] = total
        total = total + seg[g]
        over_of.append(over)
        over_sm[g] = over
        over = over + jnp.maximum(seg[g] - DIRECT, 0)
    over_of.append(over)
    mine = jnp.int32(0)
    for d in range(N_DP):
        b = (s + d) % N_DP
        at = jnp.int32(0)
        for j in range(N_DP):
            at = at + jnp.where(bucket_of[j] == b, j, 0)
        if d == 0:
            mine = at
        inv_sm[d] = at
        slot_sm[d] = starts_sm[(at - s + N_DP) % N_DP]

    def plan_over(k, carry):
        tile, of = jnp.int32(0), jnp.int32(0)
        for g in range(N_DP):
            inside = (k >= over_of[g]) & (k < over_of[g + 1])
            tile = tile + jnp.where(inside, start_of[g] + DIRECT + k - over_of[g], 0)
            of = of + jnp.where(inside, g, 0)
        tile_sm[k] = tile
        seg_sm[k] = of
        return carry

    lax.fori_loop(0, relayed, plan_over, 0)
    ends, begins, overs = [], [], []
    total = jnp.int32(0)
    for r in range(N_DP):
        begins.append(total)
        overs.append(over_sm[(mine - r + N_DP) % N_DP])
        total = total + seg[(mine - r + N_DP) % N_DP]
        ends.append(total)

    def plan_tile(k, first):
        begins_here = breaks[s, k] == 1
        pick = jnp.int32(0)
        for r in range(N_DP):
            begins_here = begins_here | (start_of[r] == k)
            inside = (k >= begins[r]) & (k < ends[r])
            within = k - begins[r]
            place = jnp.where(within < DIRECT, r * DIRECT + within,
                              N_DP * DIRECT + overs[r] + within - DIRECT)
            pick = pick + jnp.where(inside, place, 0)
        first = jnp.where(begins_here, k, first)
        first_sm[k] = first
        pick_sm[k] = pick
        return first

    lax.fori_loop(0, NBLK, plan_tile, jnp.int32(0))

    lane = lax.broadcasted_iota(jnp.int32, (LAT, BLK), 1)
    wts[:, : 2 * BLK] = kv_up[:, : 2 * BLK]
    turned = pltpu.roll(kv_up[:, 2 * BLK : 3 * BLK].astype(jnp.float32), HALF, 1)
    wts[:, 2 * BLK : 3 * BLK] = jnp.where(lane < HALF, 0.0, turned).astype(jnp.bfloat16)
    wts[:, 3 * BLK : 4 * BLK] = jnp.where(lane < HALF, turned, 0.0).astype(jnp.bfloat16)
    wts[:, 4 * BLK :] = kv_up[:, 3 * BLK :]
    kext[:, :LEAD, :] = jnp.zeros((2, LEAD, 2 * BLK), jnp.bfloat16)
    vext[:, :LEAD, :BLK] = jnp.zeros((2, LEAD, BLK), jnp.bfloat16)
    vext[:, :, BLK:] = jnp.ones((2, LEAD + NBLK * BLK, BLK), jnp.bfloat16)

    lane4 = lax.broadcasted_iota(jnp.int32, (NX * NC * HALF, BLK), 1)

    def project(half, held, chips):
        block = held[...].reshape(NX * NC * HALF, XW)
        rot = block[:, LAT:].astype(jnp.float32)
        kv = jnp.dot(block[:, :LAT], wts[...], preferred_element_type=jnp.float32)
        k0 = kv[:, :BLK].astype(jnp.bfloat16)
        r0 = jnp.where(lane4 < HALF, rot, 0.0).astype(jnp.bfloat16)
        v0 = kv[:, BLK : 2 * BLK].astype(jnp.bfloat16)
        k1 = kv[:, 2 * BLK : 3 * BLK].astype(jnp.bfloat16)
        r1 = jnp.where(lane4 < HALF, kv[:, 3 * BLK : 4 * BLK], rot).astype(jnp.bfloat16)
        v1 = kv[:, 4 * BLK :].astype(jnp.bfloat16)
        for p in range(NX):
            for q in range(NC):
                chip = chips * NX + p if half == 0 else p * NX + chips
                begin = LEAD + (chip * NC + q) * BLK + half * HALF
                at = pl.ds(pl.multiple_of(begin, HALF), HALF)
                of = slice((p * NC + q) * HALF, (p * NC + q + 1) * HALF)
                kext[0, at, :BLK] = k0[of]
                kext[0, at, BLK:] = r0[of]
                vext[0, at, :BLK] = v0[of]
                kext[1, at, :BLK] = k1[of]
                kext[1, at, BLK:] = r1[of]
                vext[1, at, :BLK] = v1[of]

    def pass_on(d):
        for half in range(2):
            for p in range(4):
                ph2_copy(half, d, p).wait_recv()
            sib_copy(half, d).start()

    def take_in(d):
        for half in range(2):
            got = (xa if half == 0 else xb)[d].at[:, 1 - c]
            remote(got, got, sib_send.at[half, d], sib_recv.at[half, d], seq=sibling).wait_recv()
            project(half, (xa if half == 0 else xb)[d], (((y + NY) if half == 0 else (x + NX)) - d) % 4)

    take_in(0)
    pass_on(1)
    pass_on(3)
    take_in(1)
    pass_on(2)
    q_start(1)
    take_in(3)
    take_in(2)
    q_start(2)
    q_start(3)

    row_id = lax.broadcasted_iota(jnp.int32, (HALF, BLK), 0)
    col_id = lax.broadcasted_iota(jnp.int32, (HALF, BLK), 1)
    none = jnp.zeros((HALF, BLK), jnp.bfloat16)

    def attend(r):
        h, half = r // 2, r % 2
        causal = col_id <= row_id + half * HALF

        def body(i, carry):
            of = pl.ds(GROUP * i, GROUP)
            if h == 0:
                q = qa[half, of]
            else:
                q = jnp.concatenate([qa[half, of, :, BLK:], qb[half, of]], axis=2)
            at = pl.ds(pl.multiple_of(i * GROUP * BLK, BLK), KEYS)
            sc = lax.dot_general(q.reshape(GROUP * HALF, 2 * BLK), kext[h, at, :],
                                 (((1,), (1,)), ((), ())), preferred_element_type=jnp.float32)
            parts = []
            for t in range(GROUP):
                part = sc[t * HALF : (t + 1) * HALF]
                low = first_sm[GROUP * i + t] - (GROUP * i - (SEG_MOST - 1))
                tiles = []
                for u in range(t, t + SEG_MOST):
                    tile = part[:, u * BLK : (u + 1) * BLK]
                    ok = causal if u == t + SEG_MOST - 1 else (low <= u)
                    tiles.append(jnp.where(ok, tile, NEG))
                top = functools.reduce(jnp.maximum, tiles)
                top = jnp.max(top, axis=1, keepdims=True)
                w = [jnp.exp2((e - top) * EXP_SCALE).astype(jnp.bfloat16) for e in tiles]
                parts.append(jnp.concatenate([none] * t + w + [none] * (GROUP - 1 - t), axis=1))
            o = jnp.dot(jnp.concatenate(parts, axis=0), vext[h, at, :],
                        preferred_element_type=jnp.float32)
            o = (o[:, :BLK] / o[:, BLK:]).astype(jnp.bfloat16)
            att[r, of] = o.reshape(GROUP, HALF, BLK)
            return carry

        lax.fori_loop(0, NBLK // GROUP, body, 0, unroll=2)

    rest = (relayed - N_DP) * HALF // N_DP

    def z_copy(r, d, source):
        return remote(zsend.at[r, d], zrecv[r].at[pl.ds(source * DIRECT, DIRECT)],
                      z_send.at[r, d], z_recv.at[r, d], dp=(s + d) % N_DP)

    def r_copy(r, d, source):
        return remote(rsend.at[r, d], rrecv[r].at[source], r_send.at[r, d], r_recv.at[r, d],
                      dp=(s + d) % N_DP)

    def f_places(r, relay):
        places = [zrecv[r].at[N_DP * DIRECT + relay]]
        if rest:
            part = pl.ds(pl.multiple_of(relay % 2 * rest, rest), rest)
            places.append(zrecv[r].at[N_DP * DIRECT + N_DP + relay // 2, part])
        return places

    def f_copies(r, d, relay):
        places = f_places(r, relay)
        pieces = [fsend.at[r, d, pl.ds(0, HALF)]]
        if rest:
            pieces.append(fsend.at[r, d, pl.ds(HALF, rest)])
        return [remote(a, b, f_send.at[r, e, d], f_recv.at[r, e, d], dp=(s + d) % N_DP)
                for e, (a, b) in enumerate(zip(pieces, places))]

    def send_relays(r):
        for d in Z_ORDER:
            relay = (s + d) % N_DP
            dst = rrecv[r].at[s] if d == 0 else rsend.at[r, d]
            dst[:HALF] = att[r, tile_sm[relay]]
            if rest:
                part = pl.ds(pl.multiple_of(relay % 2 * rest, rest), rest)
                dst[HALF:] = att[r, tile_sm[N_DP + relay // 2], part]
            if d:
                r_copy(r, d, s).start()

    def send_dp(r):
        for d in Z_ORDER:
            base = slot_sm[d]
            for j in range(DIRECT):
                tile = att[r, jnp.minimum(base + j, NBLK - 1)]
                if d == 0:
                    zrecv[r][s * DIRECT + j] = tile
                else:
                    zsend[r, d, j] = tile
            if d:
                z_copy(r, d, s).start()

    def forward(r):
        for d in range(1, N_DP):
            r_copy(r, d, (s + N_DP - d) % N_DP).wait_recv()
        for d in Z_ORDER:
            source = (inv_sm[d] - seg_sm[s] + N_DP) % N_DP
            tile = rrecv[r][source, :HALF]
            if rest:
                source = (inv_sm[d] - seg_sm[N_DP + s // 2] + N_DP) % N_DP
                more = rrecv[r][source, HALF:]
            if d:
                fsend[r, d, :HALF] = tile
                if rest:
                    fsend[r, d, HALF:] = more
                for cp in f_copies(r, d, s):
                    cp.start()
            else:
                places = f_places(r, s)
                places[0][...] = tile
                if rest:
                    places[1][...] = more

    def o_part(r, owner):
        begin = pl.multiple_of((2 * owner + r // 2) * BLK, BLK)
        return out.at[pl.ds(r % 2 * HALF, HALF), pl.ds(begin, BLK)]

    def o_copy(r, o, owner, peer):
        return remote(osend.at[r, o], o_part(r, owner), o_send.at[r, o], o_recv.at[r, o], seq=peer)

    def o_own(r):
        return pltpu.make_async_copy(osend.at[r, 0], o_part(r, me), own_sem.at[ROUNDS + r])

    def send_seq(r):
        for d in range(1, N_DP):
            z_copy(r, d, (s + N_DP - d) % N_DP).wait_recv()
            for cp in f_copies(r, d, (s + N_DP - d) % N_DP):
                cp.wait_recv()
        for o in ORDER:
            peer = seq_peer(y, x, c, o)
            osend[r, o] = zrecv[r][pick_sm[peer]]
            o_copy(r, o, me, peer).start()
        osend[r, 0] = zrecv[r][pick_sm[me]]
        o_own(r).start()

    for r in range(ROUNDS):
        q_arrive(r)
        attend(r)
        send_relays(r)
        if r != 1:
            send_dp(max(r - 1, 0))
        if r:
            forward(r - 1)
    send_dp(ROUNDS - 1)
    send_seq(0)
    forward(ROUNDS - 1)
    for r in range(1, ROUNDS):
        send_seq(r)

    for half in range(2):
        for d in range(4):
            sib_copy(half, d).wait_send()
        for d in NEAR:
            ph1_copy(half, d, y if half else x).wait_send()
            for p in range(4):
                ph2_copy(half, d, p).wait_send()
    for r in range(ROUNDS):
        q_drain(r)
        for d in range(1, N_DP):
            for cp in [z_copy(r, d, s), r_copy(r, d, s)] + f_copies(r, d, s):
                cp.wait_send()
        o_own(r).wait()

        def body(o, carry):
            cp = o_copy(r, o, seq_source(y, x, c, o), seq_peer(y, x, c, o))
            cp.wait_send()
            cp.wait_recv()
            return carry

        lax.fori_loop(1, N_SEQ, body, 0)


def call(relayed, index):
    bf16 = jnp.bfloat16
    piece = HALF + (relayed - N_DP) * HALF // N_DP
    vmem = pl.BlockSpec(memory_space=pltpu.VMEM)
    smem = pl.BlockSpec(memory_space=pltpu.SMEM)
    anywhere = pl.BlockSpec(memory_space=pl.ANY)
    dma = pltpu.SemaphoreType.DMA
    return pl.pallas_call(
        functools.partial(kernel, relayed),
        out_shape=jax.ShapeDtypeStruct((BLK, N_SEQ * 2 * HD_V), bf16),
        in_specs=[anywhere, vmem, vmem, vmem, vmem, smem, smem, smem],
        out_specs=anywhere,
        scratch_shapes=[
            *[pltpu.VMEM((NX, NC, HALF, XW), bf16)] * 8,
            pltpu.VMEM((2, NBLK, HALF, 2 * BLK), bf16),
            pltpu.VMEM((2, NBLK, HALF, BLK), bf16),
            pltpu.VMEM((LAT, 5 * BLK), bf16),
            pltpu.VMEM((2, LEAD + NBLK * BLK, 2 * BLK), bf16),
            pltpu.VMEM((2, LEAD + NBLK * BLK, 2 * BLK), bf16),
            pltpu.VMEM((ROUNDS, NBLK, HALF, BLK), bf16),
            pltpu.VMEM((ROUNDS, N_DP, DIRECT, HALF, BLK), bf16),
            *[pltpu.VMEM((N_DP * DIRECT + relayed, HALF, BLK), bf16)] * ROUNDS,
            pltpu.VMEM((ROUNDS, N_DP, piece, BLK), bf16),
            *[pltpu.VMEM((N_DP, piece, BLK), bf16)] * ROUNDS,
            pltpu.VMEM((ROUNDS, N_DP, piece, BLK), bf16),
            pltpu.VMEM((ROUNDS, N_SEQ, HALF, BLK), bf16),
            *[pltpu.SMEM((n,), jnp.int32)
              for n in (N_DP, NBLK, NBLK, N_DP, N_DP, relayed, relayed, N_DP)],
            dma((2, 4)), dma((2, 4)), dma((2, 4, 4)), dma((2, 4, 4)), dma((2, 4)), dma((2, 4)),
            dma((ROUNDS, N_SEQ)), dma((ROUNDS, N_SEQ)),
            dma((ROUNDS, N_DP)), dma((ROUNDS, N_DP)),
            dma((ROUNDS, N_DP)), dma((ROUNDS, N_DP)),
            dma((ROUNDS, 2, N_DP)), dma((ROUNDS, 2, N_DP)),
            dma((ROUNDS, N_SEQ)), dma((ROUNDS, N_SEQ)),
            dma((2 * ROUNDS,)),
        ],
        compiler_params=pltpu.CompilerParams(
            collective_id=index, has_side_effects=True, vmem_limit_bytes=56 * 2**20
        ),
    )


def on_device(queries, kv_latent, key_rope, kv_gain, kv_up, segment_blocks, bucket_of, doc_breaks):
    over = jnp.sum(jnp.maximum(segment_blocks - DIRECT, 0))
    return lax.cond(
        over <= RELAYS[0], call(RELAYS[0], 0), call(RELAYS[1], 1),
        queries, kv_latent, key_rope.T, kv_gain.reshape(1, LAT), kv_up, segment_blocks, bucket_of, doc_breaks,
    )


def solution(mesh):
    in_specs = (
        P(("dp", "seq"), None),
        P(("dp", "seq"), None),
        P(("dp", "seq"), None),
        P(),
        P(None, "seq"),
        P(),
        P(),
        P(),
    )
    return jax.shard_map(
        on_device, mesh=mesh, in_specs=in_specs, out_specs=P(("dp", "seq"), None), check_vma=False
    )
```

```python
import functools
import math

import jax
import jax.numpy as jnp
from jax import lax
from jax.experimental import pallas as pl
from jax.experimental.pallas import tpu as pltpu
from jax.sharding import PartitionSpec as P

HD_NOPE = 128
HD_ROPE = 64
HD_V = 128
BLK = 128
HALF = BLK // 2
LAT = 512
NBLK = 32
N_DP = 8
SEG_MOST = 8
NY, NX, NC = 4, 4, 2
N_SEQ = NY * NX * NC
LEAD = (SEG_MOST - 1) * BLK
GROUP = 4
KEYS = LEAD + GROUP * BLK
XW = LAT + 2 * HD_ROPE
ROUNDS = 4
ORDER = (20, 21, 12, 24, 13, 25, 18, 6, 19, 7, 22, 2, 23, 3, 28, 8, 29, 9, 4, 16, 5, 17, 10, 30, 11, 31, 14, 26, 15, 27, 1)
Z_ORDER = (4, 3, 5, 2, 6, 1, 7, 0)
EARLY = 10
NEAR = (1, 3, 2)
DIRECT = 4
RELAYS = (8, 12)
EPS = 1e-06
NEG = -1e30
EXP_SCALE = (HD_NOPE + HD_ROPE) ** -0.5 * math.log2(math.e)


def seq_peer(y, x, c, o):
    dc, dx, dy = o % NC, (o // NC) % NX, o // (NC * NX)
    return ((y + dy) % NY) * (NX * NC) + ((x + dx) % NX) * NC + (c + dc) % NC


def seq_source(y, x, c, o):
    dc, dx, dy = o % NC, (o // NC) % NX, o // (NC * NX)
    return ((y + NY - dy) % NY) * (NX * NC) + ((x + NX - dx) % NX) * NC + (c + NC - dc) % NC


def kernel(
    relayed,
    queries, latent, rope_t, gain, kv_up, seg, bucket_of, breaks,
    out,
    xa0, xa1, xa2, xa3, xb0, xb1, xb2, xb3, qa, qb, wts, kext, vext, att, zsend, zrecv0, zrecv1, zrecv2, zrecv3, rsend, rrecv0, rrecv1, rrecv2, rrecv3, fsend, osend,
    starts_sm, first_sm, pick_sm, slot_sm, over_sm, tile_sm, seg_sm, inv_sm,
    l1_send, l1_recv, l2_send, l2_recv, sib_send, sib_recv,
    q_send, q_recv, z_send, z_recv, r_send, r_recv, f_send, f_recv, o_send, o_recv, own_sem,
):
    s = lax.axis_index("dp")
    me = lax.axis_index("seq")
    y, x, c = me // (NX * NC), (me // NC) % NX, me % NC

    def remote(src, dst, send, recv, **axes):
        return pltpu.make_async_remote_copy(
            src_ref=src, dst_ref=dst, send_sem=send, recv_sem=recv,
            device_id=axes, device_id_type=pl.DeviceIdType.MESH,
        )

    xa, xb = (xa0, xa1, xa2, xa3), (xb0, xb1, xb2, xb3)
    zrecv = (zrecv0, zrecv1, zrecv2, zrecv3)
    rrecv = (rrecv0, rrecv1, rrecv2, rrecv3)

    barrier = pltpu.get_barrier_semaphore()

    def greet_seq(o, carry):
        pl.semaphore_signal(barrier, inc=1, device_id={"seq": seq_peer(y, x, c, o)},
                            device_id_type=pl.DeviceIdType.MESH)
        return carry

    lax.fori_loop(1, N_SEQ, greet_seq, 0)
    for d in range(1, N_DP):
        pl.semaphore_signal(barrier, inc=1, device_id={"dp": (s + d) % N_DP},
                            device_id_type=pl.DeviceIdType.MESH)

    lat = latent[...].astype(jnp.float32)
    normed = (
        lat * lax.rsqrt(jnp.mean(lat * lat, axis=1, keepdims=True) + EPS) * gain[...]
    ).astype(jnp.bfloat16)
    rope = rope_t[...].astype(jnp.float32)
    rope2 = jnp.transpose(jnp.concatenate([rope, rope], axis=0)).astype(jnp.bfloat16)
    rows = jnp.concatenate([normed, rope2], axis=1)
    xa0[x, c] = rows[:HALF]
    xb0[y, c] = rows[HALF:]

    pl.semaphore_wait(barrier, N_SEQ - 1 + N_DP - 1)

    def at_x(d):
        return y * (NX * NC) + ((x + d) % NX) * NC + c

    def at_y(d):
        return ((y + d) % NY) * (NX * NC) + x * NC + c

    sibling = y * (NX * NC) + x * NC + (1 - c)
    def ph1_copy(half, d, place):
        ref = xa0.at[place, c] if half == 0 else xb0.at[place, c]
        return remote(ref, ref, l1_send.at[half, d], l1_recv.at[half, d], seq=at_x(d) if half == 0 else at_y(d))

    def ph2_copy(half, d, p):
        if half == 0:
            place = (x + NX - p) % NX
            src, dst, peer = xa0.at[place, c], xa[d].at[place, c], at_y(d)
        else:
            place = (y + NY - p) % NY
            src, dst, peer = xb0.at[place, c], xb[d].at[place, c], at_x(d)
        return remote(src, dst, l2_send.at[half, d, p], l2_recv.at[half, d, p], seq=peer)

    def sib_copy(half, d):
        ref = (xa if half == 0 else xb)[d].at[:, c]
        return remote(ref, ref, sib_send.at[half, d], sib_recv.at[half, d], seq=sibling)

    for d in NEAR:
        ph1_copy(0, d, x).start()
        ph1_copy(1, d, y).start()
    for d in NEAR:
        ph2_copy(0, d, 0).start()
        ph2_copy(1, d, 0).start()

    def q_copy(r, o, peer, slot):
        h, half = r // 2, r % 2
        width = BLK if h else 2 * BLK
        begin = pl.multiple_of(peer * (3 * BLK) + h * 2 * BLK, BLK)
        return remote(queries.at[pl.ds(half * HALF, HALF), pl.ds(begin, width)],
                      (qb if h else qa).at[half, slot], q_send.at[r], q_recv.at[r], seq=peer)

    def q_start(r, order=ORDER):
        for o in order:
            q_copy(r, o, seq_peer(y, x, c, o), me).start()

    def all_of(ref, sem):
        part = ref.at[pl.ds(0, N_SEQ - 1)]
        return pltpu.make_async_copy(part, part, sem)

    def q_arrive(r):
        q_own(r).wait()
        all_of((qb if r // 2 else qa).at[r % 2], q_recv.at[r]).wait()

    def q_drain(r):
        all_of((qb if r // 2 else qa).at[r % 2], q_send.at[r]).wait()

    def q_own(r):
        h, half = r // 2, r % 2
        width = BLK if h else 2 * BLK
        begin = pl.multiple_of(me * (3 * BLK) + h * 2 * BLK, BLK)
        return pltpu.make_async_copy(queries.at[pl.ds(half * HALF, HALF), pl.ds(begin, width)],
                                     (qb if h else qa).at[half, me], own_sem.at[r])

    q_start(0, ORDER[:EARLY])
    for r in range(ROUNDS):
        q_own(r).start()

    for p in NEAR:
        ph1_copy(0, p, (x + NX - p) % NX).wait_recv()
        for d in NEAR:
            ph2_copy(0, d, p).start()
        ph1_copy(1, p, (y + NY - p) % NY).wait_recv()
        for d in NEAR:
            ph2_copy(1, d, p).start()
    for half in range(2):
        sib_copy(half, 0).start()

    q_start(0, ORDER[EARLY:])

    total, over = jnp.int32(0), jnp.int32(0)
    start_of, over_of = [], []
    for g in range(N_DP):
        start_of.append(total)
        starts_sm[g] = total
        total = total + seg[g]
        over_of.append(over)
        over_sm[g] = over
        over = over + jnp.maximum(seg[g] - DIRECT, 0)
    over_of.append(over)
    mine = jnp.int32(0)
    for d in range(N_DP):
        b = (s + d) % N_DP
        at = jnp.int32(0)
        for j in range(N_DP):
            at = at + jnp.where(bucket_of[j] == b, j, 0)
        if d == 0:
            mine = at
        inv_sm[d] = at
        slot_sm[d] = starts_sm[(at - s + N_DP) % N_DP]

    def plan_over(k, carry):
        tile, of = jnp.int32(0), jnp.int32(0)
        for g in range(N_DP):
            inside = (k >= over_of[g]) & (k < over_of[g + 1])
            tile = tile + jnp.where(inside, start_of[g] + DIRECT + k - over_of[g], 0)
            of = of + jnp.where(inside, g, 0)
        tile_sm[k] = tile
        seg_sm[k] = of
        return carry

    lax.fori_loop(0, relayed, plan_over, 0)
    ends, begins, overs = [], [], []
    total = jnp.int32(0)
    for r in range(N_DP):
        begins.append(total)
        overs.append(over_sm[(mine - r + N_DP) % N_DP])
        total = total + seg[(mine - r + N_DP) % N_DP]
        ends.append(total)

    def plan_tile(k, first):
        begins_here = breaks[s, k] == 1
        pick = jnp.int32(0)
        for r in range(N_DP):
            begins_here = begins_here | (start_of[r] == k)
            inside = (k >= begins[r]) & (k < ends[r])
            within = k - begins[r]
            place = jnp.where(within < DIRECT, r * DIRECT + within,
                              N_DP * DIRECT + overs[r] + within - DIRECT)
            pick = pick + jnp.where(inside, place, 0)
        first = jnp.where(begins_here, k, first)
        first_sm[k] = first
        pick_sm[k] = pick
        return first

    lax.fori_loop(0, NBLK, plan_tile, jnp.int32(0))

    lane = lax.broadcasted_iota(jnp.int32, (LAT, BLK), 1)
    wts[:, : 2 * BLK] = kv_up[:, : 2 * BLK]
    turned = pltpu.roll(kv_up[:, 2 * BLK : 3 * BLK].astype(jnp.float32), HALF, 1)
    wts[:, 2 * BLK : 3 * BLK] = jnp.where(lane < HALF, 0.0, turned).astype(jnp.bfloat16)
    wts[:, 3 * BLK : 4 * BLK] = jnp.where(lane < HALF, turned, 0.0).astype(jnp.bfloat16)
    wts[:, 4 * BLK :] = kv_up[:, 3 * BLK :]
    kext[:, :LEAD, :] = jnp.zeros((2, LEAD, 2 * BLK), jnp.bfloat16)
    vext[:, :LEAD, :BLK] = jnp.zeros((2, LEAD, BLK), jnp.bfloat16)
    vext[:, :, BLK:] = jnp.ones((2, LEAD + NBLK * BLK, BLK), jnp.bfloat16)

    lane4 = lax.broadcasted_iota(jnp.int32, (NX * NC * HALF, BLK), 1)

    def project(half, held, chips):
        block = held[...].reshape(NX * NC * HALF, XW)
        rot = block[:, LAT:].astype(jnp.float32)
        kv = jnp.dot(block[:, :LAT], wts[...], preferred_element_type=jnp.float32)
        k0 = kv[:, :BLK].astype(jnp.bfloat16)
        r0 = jnp.where(lane4 < HALF, rot, 0.0).astype(jnp.bfloat16)
        v0 = kv[:, BLK : 2 * BLK].astype(jnp.bfloat16)
        k1 = kv[:, 2 * BLK : 3 * BLK].astype(jnp.bfloat16)
        r1 = jnp.where(lane4 < HALF, kv[:, 3 * BLK : 4 * BLK], rot).astype(jnp.bfloat16)
        v1 = kv[:, 4 * BLK :].astype(jnp.bfloat16)
        for p in range(NX):
            for q in range(NC):
                chip = chips * NX + p if half == 0 else p * NX + chips
                begin = LEAD + (chip * NC + q) * BLK + half * HALF
                at = pl.ds(pl.multiple_of(begin, HALF), HALF)
                of = slice((p * NC + q) * HALF, (p * NC + q + 1) * HALF)
                kext[0, at, :BLK] = k0[of]
                kext[0, at, BLK:] = r0[of]
                vext[0, at, :BLK] = v0[of]
                kext[1, at, :BLK] = k1[of]
                kext[1, at, BLK:] = r1[of]
                vext[1, at, :BLK] = v1[of]

    def pass_on(d):
        for half in range(2):
            for p in range(4):
                ph2_copy(half, d, p).wait_recv()
            sib_copy(half, d).start()

    def take_in(d):
        for half in range(2):
            got = (xa if half == 0 else xb)[d].at[:, 1 - c]
            remote(got, got, sib_send.at[half, d], sib_recv.at[half, d], seq=sibling).wait_recv()
            project(half, (xa if half == 0 else xb)[d], (((y + NY) if half == 0 else (x + NX)) - d) % 4)

    take_in(0)
    pass_on(1)
    pass_on(3)
    take_in(1)
    q_start(1)
    pass_on(2)
    take_in(3)
    take_in(2)

    row_id = lax.broadcasted_iota(jnp.int32, (HALF, BLK), 0)
    col_id = lax.broadcasted_iota(jnp.int32, (HALF, BLK), 1)
    none = jnp.zeros((HALF, BLK), jnp.bfloat16)

    def attend(r):
        h, half = r // 2, r % 2
        causal = col_id <= row_id + half * HALF

        def body(i, carry):
            of = pl.ds(GROUP * i, GROUP)
            if h == 0:
                q = qa[half, of]
            else:
                q = jnp.concatenate([qa[half, of, :, BLK:], qb[half, of]], axis=2)
            at = pl.ds(pl.multiple_of(i * GROUP * BLK, BLK), KEYS)
            sc = lax.dot_general(q.reshape(GROUP * HALF, 2 * BLK), kext[h, at, :],
                                 (((1,), (1,)), ((), ())), preferred_element_type=jnp.float32)
            parts = []
            for t in range(GROUP):
                part = sc[t * HALF : (t + 1) * HALF]
                low = first_sm[GROUP * i + t] - (GROUP * i - (SEG_MOST - 1))
                tiles = []
                for u in range(t, t + SEG_MOST):
                    tile = part[:, u * BLK : (u + 1) * BLK]
                    ok = causal if u == t + SEG_MOST - 1 else (low <= u)
                    tiles.append(jnp.where(ok, tile, NEG))
                top = functools.reduce(jnp.maximum, tiles)
                top = jnp.max(top, axis=1, keepdims=True)
                w = [jnp.exp2((e - top) * EXP_SCALE).astype(jnp.bfloat16) for e in tiles]
                parts.append(jnp.concatenate([none] * t + w + [none] * (GROUP - 1 - t), axis=1))
            o = jnp.dot(jnp.concatenate(parts, axis=0), vext[h, at, :],
                        preferred_element_type=jnp.float32)
            o = (o[:, :BLK] / o[:, BLK:]).astype(jnp.bfloat16)
            att[r, of] = o.reshape(GROUP, HALF, BLK)
            return carry

        lax.fori_loop(0, NBLK // GROUP, body, 0, unroll=2)

    rest = (relayed - N_DP) * HALF // N_DP

    def z_copy(r, d, source):
        return remote(zsend.at[r, d], zrecv[r].at[pl.ds(source * DIRECT, DIRECT)],
                      z_send.at[r, d], z_recv.at[r, d], dp=(s + d) % N_DP)

    def r_copy(r, d, source):
        return remote(rsend.at[r, d], rrecv[r].at[source], r_send.at[r, d], r_recv.at[r, d],
                      dp=(s + d) % N_DP)

    def f_places(r, relay):
        places = [zrecv[r].at[N_DP * DIRECT + relay]]
        if rest:
            part = pl.ds(pl.multiple_of(relay % 2 * rest, rest), rest)
            places.append(zrecv[r].at[N_DP * DIRECT + N_DP + relay // 2, part])
        return places

    def f_copies(r, d, relay):
        places = f_places(r, relay)
        pieces = [fsend.at[r, d, pl.ds(0, HALF)]]
        if rest:
            pieces.append(fsend.at[r, d, pl.ds(HALF, rest)])
        return [remote(a, b, f_send.at[r, e, d], f_recv.at[r, e, d], dp=(s + d) % N_DP)
                for e, (a, b) in enumerate(zip(pieces, places))]

    def send_relays(r):
        for d in Z_ORDER:
            relay = (s + d) % N_DP
            dst = rrecv[r].at[s] if d == 0 else rsend.at[r, d]
            dst[:HALF] = att[r, tile_sm[relay]]
            if rest:
                part = pl.ds(pl.multiple_of(relay % 2 * rest, rest), rest)
                dst[HALF:] = att[r, tile_sm[N_DP + relay // 2], part]
            if d:
                r_copy(r, d, s).start()

    def send_dp(r):
        for d in Z_ORDER:
            base = slot_sm[d]
            for j in range(DIRECT):
                tile = att[r, jnp.minimum(base + j, NBLK - 1)]
                if d == 0:
                    zrecv[r][s * DIRECT + j] = tile
                else:
                    zsend[r, d, j] = tile
            if d:
                z_copy(r, d, s).start()

    def forward(r):
        for d in range(1, N_DP):
            r_copy(r, d, (s + N_DP - d) % N_DP).wait_recv()
        for d in Z_ORDER:
            source = (inv_sm[d] - seg_sm[s] + N_DP) % N_DP
            tile = rrecv[r][source, :HALF]
            if rest:
                source = (inv_sm[d] - seg_sm[N_DP + s // 2] + N_DP) % N_DP
                more = rrecv[r][source, HALF:]
            if d:
                fsend[r, d, :HALF] = tile
                if rest:
                    fsend[r, d, HALF:] = more
                for cp in f_copies(r, d, s):
                    cp.start()
            else:
                places = f_places(r, s)
                places[0][...] = tile
                if rest:
                    places[1][...] = more

    def o_part(r, owner):
        begin = pl.multiple_of((2 * owner + r // 2) * BLK, BLK)
        return out.at[pl.ds(r % 2 * HALF, HALF), pl.ds(begin, BLK)]

    def o_copy(r, o, owner, peer):
        return remote(osend.at[r, o], o_part(r, owner), o_send.at[r], o_recv.at[r], seq=peer)

    def o_own(r):
        return pltpu.make_async_copy(osend.at[r, 0], o_part(r, me), own_sem.at[ROUNDS + r])

    def send_seq(r):
        for d in range(1, N_DP):
            z_copy(r, d, (s + N_DP - d) % N_DP).wait_recv()
            for cp in f_copies(r, d, (s + N_DP - d) % N_DP):
                cp.wait_recv()
        for o in ORDER:
            peer = seq_peer(y, x, c, o)
            osend[r, o] = zrecv[r][pick_sm[peer]]
            o_copy(r, o, me, peer).start()
        osend[r, 0] = zrecv[r][pick_sm[me]]
        o_own(r).start()

    def gather_drain():
        for half in range(2):
            for d in range(4):
                sib_copy(half, d).wait_send()
            for d in NEAR:
                ph1_copy(half, d, y if half else x).wait_send()
                for p in range(4):
                    ph2_copy(half, d, p).wait_send()

    def dp_drain(r):
        for d in range(1, N_DP):
            for cp in [z_copy(r, d, s), r_copy(r, d, s)] + f_copies(r, d, s):
                cp.wait_send()

    def o_drain(r):
        o_own(r).wait()
        all_of(osend.at[r], o_send.at[r]).wait()
        all_of(osend.at[r], o_recv.at[r]).wait()

    for r in range(ROUNDS):
        q_arrive(r)
        attend(r)
        if r:
            forward(r - 1)
        send_relays(r)
        send_dp(r)
        if r == 0:
            q_start(2)
            q_start(3)
    gather_drain()
    send_seq(0)
    forward(ROUNDS - 1)
    for r in range(ROUNDS):
        q_drain(r)
    send_seq(1)
    o_drain(0)
    send_seq(2)
    dp_drain(0)
    dp_drain(1)
    o_drain(1)
    send_seq(3)
    dp_drain(2)
    dp_drain(3)
    o_drain(2)
    o_drain(3)


def call(relayed, index):
    bf16 = jnp.bfloat16
    piece = HALF + (relayed - N_DP) * HALF // N_DP
    vmem = pl.BlockSpec(memory_space=pltpu.VMEM)
    smem = pl.BlockSpec(memory_space=pltpu.SMEM)
    anywhere = pl.BlockSpec(memory_space=pl.ANY)
    dma = pltpu.SemaphoreType.DMA
    return pl.pallas_call(
        functools.partial(kernel, relayed),
        out_shape=jax.ShapeDtypeStruct((BLK, N_SEQ * 2 * HD_V), bf16),
        in_specs=[anywhere, vmem, vmem, vmem, vmem, smem, smem, smem],
        out_specs=anywhere,
        scratch_shapes=[
            *[pltpu.VMEM((NX, NC, HALF, XW), bf16)] * 8,
            pltpu.VMEM((2, NBLK, HALF, 2 * BLK), bf16),
            pltpu.VMEM((2, NBLK, HALF, BLK), bf16),
            pltpu.VMEM((LAT, 5 * BLK), bf16),
            pltpu.VMEM((2, LEAD + NBLK * BLK, 2 * BLK), bf16),
            pltpu.VMEM((2, LEAD + NBLK * BLK, 2 * BLK), bf16),
            pltpu.VMEM((ROUNDS, NBLK, HALF, BLK), bf16),
            pltpu.VMEM((ROUNDS, N_DP, DIRECT, HALF, BLK), bf16),
            *[pltpu.VMEM((N_DP * DIRECT + relayed, HALF, BLK), bf16)] * ROUNDS,
            pltpu.VMEM((ROUNDS, N_DP, piece, BLK), bf16),
            *[pltpu.VMEM((N_DP, piece, BLK), bf16)] * ROUNDS,
            pltpu.VMEM((ROUNDS, N_DP, piece, BLK), bf16),
            pltpu.VMEM((ROUNDS, N_SEQ, HALF, BLK), bf16),
            *[pltpu.SMEM((n,), jnp.int32)
              for n in (N_DP, NBLK, NBLK, N_DP, N_DP, relayed, relayed, N_DP)],
            dma((2, 4)), dma((2, 4)), dma((2, 4, 4)), dma((2, 4, 4)), dma((2, 4)), dma((2, 4)),
            dma((ROUNDS,)), dma((ROUNDS,)),
            dma((ROUNDS, N_DP)), dma((ROUNDS, N_DP)),
            dma((ROUNDS, N_DP)), dma((ROUNDS, N_DP)),
            dma((ROUNDS, 2, N_DP)), dma((ROUNDS, 2, N_DP)),
            dma((ROUNDS,)), dma((ROUNDS,)),
            dma((2 * ROUNDS,)),
        ],
        compiler_params=pltpu.CompilerParams(
            collective_id=index, has_side_effects=True, vmem_limit_bytes=56 * 2**20
        ),
    )


def on_device(queries, kv_latent, key_rope, kv_gain, kv_up, segment_blocks, bucket_of, doc_breaks):
    over = jnp.sum(jnp.maximum(segment_blocks - DIRECT, 0))
    return lax.cond(
        over <= RELAYS[0], call(RELAYS[0], 0), call(RELAYS[1], 1),
        queries, kv_latent, key_rope.T, kv_gain.reshape(1, LAT), kv_up, segment_blocks, bucket_of, doc_breaks,
    )


def solution(mesh):
    in_specs = (
        P(("dp", "seq"), None),
        P(("dp", "seq"), None),
        P(("dp", "seq"), None),
        P(),
        P(None, "seq"),
        P(),
        P(),
        P(),
    )
    return jax.shard_map(
        on_device, mesh=mesh, in_specs=in_specs, out_specs=P(("dp", "seq"), None), check_vma=False
    )
```

```python
import functools
import math

import jax
import jax.numpy as jnp
from jax import lax
from jax.experimental import pallas as pl
from jax.experimental.pallas import tpu as pltpu
from jax.sharding import PartitionSpec as P

HD_NOPE = 128
HD_ROPE = 64
HD_V = 128
BLK = 128
HALF = BLK // 2
LAT = 512
NBLK = 32
N_DP = 8
SEG_MOST = 8
NY, NX, NC = 4, 4, 2
N_SEQ = NY * NX * NC
LEAD = (SEG_MOST - 1) * BLK
GROUP = 4
KEYS = LEAD + GROUP * BLK
XW = LAT + 2 * HD_ROPE
ROUNDS = 4
ORDER = (20, 21, 12, 24, 13, 25, 18, 6, 19, 7, 22, 2, 23, 3, 28, 8, 29, 9, 4, 16, 5, 17, 10, 30, 11, 31, 14, 26, 15, 27, 1)
Z_ORDER = (4, 3, 5, 2, 6, 1, 7, 0)
EARLY = 10
NEAR = (1, 3, 2)
DIRECT = 4
RELAYS = (8, 12)
EPS = 1e-06
NEG = -1e30
EXP_SCALE = (HD_NOPE + HD_ROPE) ** -0.5 * math.log2(math.e)


def seq_peer(y, x, c, o):
    dc, dx, dy = o % NC, (o // NC) % NX, o // (NC * NX)
    return ((y + dy) % NY) * (NX * NC) + ((x + dx) % NX) * NC + (c + dc) % NC


def seq_source(y, x, c, o):
    dc, dx, dy = o % NC, (o // NC) % NX, o // (NC * NX)
    return ((y + NY - dy) % NY) * (NX * NC) + ((x + NX - dx) % NX) * NC + (c + NC - dc) % NC


def kernel(
    relayed,
    queries, latent, rope_t, gain, kv_up, seg, bucket_of, breaks,
    out,
    xa0, xa1, xa2, xa3, xb0, xb1, xb2, xb3, qa, qb, wts, kext, vext, att, zsend, zrecv0, zrecv1, zrecv2, zrecv3, rsend, rrecv0, rrecv1, rrecv2, rrecv3, fsend, osend,
    starts_sm, first_sm, pick_sm, slot_sm, over_sm, tile_sm, seg_sm, inv_sm,
    l1_send, l1_recv, l2_send, l2_recv, sib_send, sib_recv,
    q_send, q_recv, z_send, z_recv, r_send, r_recv, f_send, f_recv, o_send, o_recv, own_sem,
):
    s = lax.axis_index("dp")
    me = lax.axis_index("seq")
    y, x, c = me // (NX * NC), (me // NC) % NX, me % NC

    def remote(src, dst, send, recv, **axes):
        return pltpu.make_async_remote_copy(
            src_ref=src, dst_ref=dst, send_sem=send, recv_sem=recv,
            device_id=axes, device_id_type=pl.DeviceIdType.MESH,
        )

    xa, xb = (xa0, xa1, xa2, xa3), (xb0, xb1, xb2, xb3)
    zrecv = (zrecv0, zrecv1, zrecv2, zrecv3)
    rrecv = (rrecv0, rrecv1, rrecv2, rrecv3)

    barrier = pltpu.get_barrier_semaphore()

    def greet_seq(o, carry):
        pl.semaphore_signal(barrier, inc=1, device_id={"seq": seq_peer(y, x, c, o)},
                            device_id_type=pl.DeviceIdType.MESH)
        return carry

    lax.fori_loop(1, N_SEQ, greet_seq, 0)
    for d in range(1, N_DP):
        pl.semaphore_signal(barrier, inc=1, device_id={"dp": (s + d) % N_DP},
                            device_id_type=pl.DeviceIdType.MESH)

    lat = latent[...].astype(jnp.float32)
    normed = (
        lat * lax.rsqrt(jnp.mean(lat * lat, axis=1, keepdims=True) + EPS) * gain[...]
    ).astype(jnp.bfloat16)
    rope = rope_t[...].astype(jnp.float32)
    rope2 = jnp.transpose(jnp.concatenate([rope, rope], axis=0)).astype(jnp.bfloat16)
    rows = jnp.concatenate([normed, rope2], axis=1)
    xa0[x, c] = rows[:HALF]
    xb0[y, c] = rows[HALF:]

    pl.semaphore_wait(barrier, N_SEQ - 1 + N_DP - 1)

    def at_x(d):
        return y * (NX * NC) + ((x + d) % NX) * NC + c

    def at_y(d):
        return ((y + d) % NY) * (NX * NC) + x * NC + c

    sibling = y * (NX * NC) + x * NC + (1 - c)
    def ph1_copy(half, d, place):
        ref = xa0.at[place, c] if half == 0 else xb0.at[place, c]
        return remote(ref, ref, l1_send.at[half, d], l1_recv.at[half, d], seq=at_x(d) if half == 0 else at_y(d))

    def ph2_copy(half, d, p):
        if half == 0:
            place = (x + NX - p) % NX
            src, dst, peer = xa0.at[place, c], xa[d].at[place, c], at_y(d)
        else:
            place = (y + NY - p) % NY
            src, dst, peer = xb0.at[place, c], xb[d].at[place, c], at_x(d)
        return remote(src, dst, l2_send.at[half, d, p], l2_recv.at[half, d, p], seq=peer)

    def sib_copy(half, d):
        ref = (xa if half == 0 else xb)[d].at[:, c]
        return remote(ref, ref, sib_send.at[half, d], sib_recv.at[half, d], seq=sibling)

    for d in NEAR:
        ph1_copy(0, d, x).start()
        ph1_copy(1, d, y).start()
    for d in NEAR:
        ph2_copy(0, d, 0).start()
        ph2_copy(1, d, 0).start()

    def q_copy(r, o, peer, slot):
        h, half = r // 2, r % 2
        width = BLK if h else 2 * BLK
        begin = pl.multiple_of(peer * (3 * BLK) + h * 2 * BLK, BLK)
        return remote(queries.at[pl.ds(half * HALF, HALF), pl.ds(begin, width)],
                      (qb if h else qa).at[half, slot], q_send.at[r], q_recv.at[r], seq=peer)

    def q_start(r, order=ORDER):
        for o in order:
            q_copy(r, o, seq_peer(y, x, c, o), me).start()

    def all_of(ref, sem, count=N_SEQ - 1):
        part = ref.at[pl.ds(0, count)]
        return pltpu.make_async_copy(part, part, sem)

    def q_arrive(r):
        q_own(r).wait()
        all_of((qb if r // 2 else qa).at[r % 2], q_recv.at[r]).wait()

    def q_drain(r):
        all_of((qb if r // 2 else qa).at[r % 2], q_send.at[r]).wait()

    def q_own(r):
        h, half = r // 2, r % 2
        width = BLK if h else 2 * BLK
        begin = pl.multiple_of(me * (3 * BLK) + h * 2 * BLK, BLK)
        return pltpu.make_async_copy(queries.at[pl.ds(half * HALF, HALF), pl.ds(begin, width)],
                                     (qb if h else qa).at[half, me], own_sem.at[r])

    q_start(0, ORDER[:EARLY])
    for r in range(ROUNDS):
        q_own(r).start()

    for p in NEAR:
        ph1_copy(0, p, (x + NX - p) % NX).wait_recv()
        for d in NEAR:
            ph2_copy(0, d, p).start()
        ph1_copy(1, p, (y + NY - p) % NY).wait_recv()
        for d in NEAR:
            ph2_copy(1, d, p).start()
    for half in range(2):
        sib_copy(half, 0).start()

    q_start(0, ORDER[EARLY:])

    total, over = jnp.int32(0), jnp.int32(0)
    start_of, over_of = [], []
    for g in range(N_DP):
        start_of.append(total)
        starts_sm[g] = total
        total = total + seg[g]
        over_of.append(over)
        over_sm[g] = over
        over = over + jnp.maximum(seg[g] - DIRECT, 0)
    over_of.append(over)
    mine = jnp.int32(0)
    for d in range(N_DP):
        b = (s + d) % N_DP
        at = jnp.int32(0)
        for j in range(N_DP):
            at = at + jnp.where(bucket_of[j] == b, j, 0)
        if d == 0:
            mine = at
        inv_sm[d] = at
        slot_sm[d] = starts_sm[(at - s + N_DP) % N_DP]

    def plan_over(k, carry):
        tile, of = jnp.int32(0), jnp.int32(0)
        for g in range(N_DP):
            inside = (k >= over_of[g]) & (k < over_of[g + 1])
            tile = tile + jnp.where(inside, start_of[g] + DIRECT + k - over_of[g], 0)
            of = of + jnp.where(inside, g, 0)
        tile_sm[k] = tile
        seg_sm[k] = of
        return carry

    lax.fori_loop(0, relayed, plan_over, 0)
    ends, begins, overs = [], [], []
    total = jnp.int32(0)
    for r in range(N_DP):
        begins.append(total)
        overs.append(over_sm[(mine - r + N_DP) % N_DP])
        total = total + seg[(mine - r + N_DP) % N_DP]
        ends.append(total)

    def plan_tile(k, first):
        begins_here = breaks[s, k] == 1
        pick = jnp.int32(0)
        for r in range(N_DP):
            begins_here = begins_here | (start_of[r] == k)
            inside = (k >= begins[r]) & (k < ends[r])
            within = k - begins[r]
            place = jnp.where(within < DIRECT, r * DIRECT + within,
                              N_DP * DIRECT + overs[r] + within - DIRECT)
            pick = pick + jnp.where(inside, place, 0)
        first = jnp.where(begins_here, k, first)
        first_sm[k] = first
        pick_sm[k] = pick
        return first

    lax.fori_loop(0, NBLK, plan_tile, jnp.int32(0))

    lane = lax.broadcasted_iota(jnp.int32, (LAT, BLK), 1)
    wts[:, : 2 * BLK] = kv_up[:, : 2 * BLK]
    turned = pltpu.roll(kv_up[:, 2 * BLK : 3 * BLK].astype(jnp.float32), HALF, 1)
    wts[:, 2 * BLK : 3 * BLK] = jnp.where(lane < HALF, 0.0, turned).astype(jnp.bfloat16)
    wts[:, 3 * BLK : 4 * BLK] = jnp.where(lane < HALF, turned, 0.0).astype(jnp.bfloat16)
    wts[:, 4 * BLK :] = kv_up[:, 3 * BLK :]
    kext[:, :LEAD, :] = jnp.zeros((2, LEAD, 2 * BLK), jnp.bfloat16)
    vext[:, :LEAD, :BLK] = jnp.zeros((2, LEAD, BLK), jnp.bfloat16)
    vext[:, :, BLK:] = jnp.ones((2, LEAD + NBLK * BLK, BLK), jnp.bfloat16)

    lane4 = lax.broadcasted_iota(jnp.int32, (NX * NC * HALF, BLK), 1)

    def project(half, held, chips):
        block = held[...].reshape(NX * NC * HALF, XW)
        rot = block[:, LAT:].astype(jnp.float32)
        kv = jnp.dot(block[:, :LAT], wts[...], preferred_element_type=jnp.float32)
        k0 = kv[:, :BLK].astype(jnp.bfloat16)
        r0 = jnp.where(lane4 < HALF, rot, 0.0).astype(jnp.bfloat16)
        v0 = kv[:, BLK : 2 * BLK].astype(jnp.bfloat16)
        k1 = kv[:, 2 * BLK : 3 * BLK].astype(jnp.bfloat16)
        r1 = jnp.where(lane4 < HALF, kv[:, 3 * BLK : 4 * BLK], rot).astype(jnp.bfloat16)
        v1 = kv[:, 4 * BLK :].astype(jnp.bfloat16)
        for p in range(NX):
            for q in range(NC):
                chip = chips * NX + p if half == 0 else p * NX + chips
                begin = LEAD + (chip * NC + q) * BLK + half * HALF
                at = pl.ds(pl.multiple_of(begin, HALF), HALF)
                of = slice((p * NC + q) * HALF, (p * NC + q + 1) * HALF)
                kext[0, at, :BLK] = k0[of]
                kext[0, at, BLK:] = r0[of]
                vext[0, at, :BLK] = v0[of]
                kext[1, at, :BLK] = k1[of]
                kext[1, at, BLK:] = r1[of]
                vext[1, at, :BLK] = v1[of]

    def pass_on(d):
        for half in range(2):
            for p in range(4):
                ph2_copy(half, d, p).wait_recv()
            sib_copy(half, d).start()

    def take_in(d):
        for half in range(2):
            got = (xa if half == 0 else xb)[d].at[:, 1 - c]
            remote(got, got, sib_send.at[half, d], sib_recv.at[half, d], seq=sibling).wait_recv()
            project(half, (xa if half == 0 else xb)[d], (((y + NY) if half == 0 else (x + NX)) - d) % 4)

    take_in(0)
    pass_on(1)
    pass_on(3)
    take_in(1)
    q_start(1)
    pass_on(2)
    take_in(3)
    take_in(2)

    row_id = lax.broadcasted_iota(jnp.int32, (HALF, BLK), 0)
    col_id = lax.broadcasted_iota(jnp.int32, (HALF, BLK), 1)
    none = jnp.zeros((HALF, BLK), jnp.bfloat16)

    def attend(r):
        h, half = r // 2, r % 2
        causal = col_id <= row_id + half * HALF

        def body(i, carry):
            of = pl.ds(GROUP * i, GROUP)
            if h == 0:
                q = qa[half, of]
            else:
                q = jnp.concatenate([qa[half, of, :, BLK:], qb[half, of]], axis=2)
            at = pl.ds(pl.multiple_of(i * GROUP * BLK, BLK), KEYS)
            sc = lax.dot_general(q.reshape(GROUP * HALF, 2 * BLK), kext[h, at, :],
                                 (((1,), (1,)), ((), ())), preferred_element_type=jnp.float32)
            parts = []
            for t in range(GROUP):
                part = sc[t * HALF : (t + 1) * HALF]
                low = first_sm[GROUP * i + t] - (GROUP * i - (SEG_MOST - 1))
                tiles = []
                for u in range(t, t + SEG_MOST):
                    tile = part[:, u * BLK : (u + 1) * BLK]
                    ok = causal if u == t + SEG_MOST - 1 else (low <= u)
                    tiles.append(jnp.where(ok, tile, NEG))
                top = functools.reduce(jnp.maximum, tiles)
                top = jnp.max(top, axis=1, keepdims=True)
                w = [jnp.exp2((e - top) * EXP_SCALE).astype(jnp.bfloat16) for e in tiles]
                parts.append(jnp.concatenate([none] * t + w + [none] * (GROUP - 1 - t), axis=1))
            o = jnp.dot(jnp.concatenate(parts, axis=0), vext[h, at, :],
                        preferred_element_type=jnp.float32)
            o = (o[:, :BLK] / o[:, BLK:]).astype(jnp.bfloat16)
            att[r, of] = o.reshape(GROUP, HALF, BLK)
            return carry

        lax.fori_loop(0, NBLK // GROUP, body, 0, unroll=2)

    rest = (relayed - N_DP) * HALF // N_DP

    def z_copy(r, d, source):
        return remote(zsend.at[r, d], zrecv[r].at[pl.ds(source * DIRECT, DIRECT)],
                      z_send.at[r], z_recv.at[r], dp=(s + d) % N_DP)

    def r_copy(r, d, source):
        return remote(rsend.at[r, d], rrecv[r].at[source], r_send.at[r], r_recv.at[r],
                      dp=(s + d) % N_DP)

    def f_places(r, relay):
        places = [zrecv[r].at[N_DP * DIRECT + relay]]
        if rest:
            part = pl.ds(pl.multiple_of(relay % 2 * rest, rest), rest)
            places.append(zrecv[r].at[N_DP * DIRECT + N_DP + relay // 2, part])
        return places

    def f_copies(r, d, relay):
        places = f_places(r, relay)
        pieces = [fsend.at[r, d, pl.ds(0, HALF)]]
        if rest:
            pieces.append(fsend.at[r, d, pl.ds(HALF, rest)])
        return [remote(a, b, f_send.at[r], f_recv.at[r], dp=(s + d) % N_DP)
                for a, b in zip(pieces, places)]

    def send_relays(r):
        for d in Z_ORDER:
            relay = (s + d) % N_DP
            dst = rrecv[r].at[s] if d == 0 else rsend.at[r, d]
            dst[:HALF] = att[r, tile_sm[relay]]
            if rest:
                part = pl.ds(pl.multiple_of(relay % 2 * rest, rest), rest)
                dst[HALF:] = att[r, tile_sm[N_DP + relay // 2], part]
            if d:
                r_copy(r, d, s).start()

    def send_dp(r):
        for d in Z_ORDER:
            base = slot_sm[d]
            for j in range(DIRECT):
                tile = att[r, jnp.minimum(base + j, NBLK - 1)]
                if d == 0:
                    zrecv[r][s * DIRECT + j] = tile
                else:
                    zsend[r, d, j] = tile
            if d:
                z_copy(r, d, s).start()

    def forward(r):
        all_of(rsend.at[r], r_recv.at[r], N_DP - 1).wait()
        for d in Z_ORDER:
            source = (inv_sm[d] - seg_sm[s] + N_DP) % N_DP
            tile = rrecv[r][source, :HALF]
            if rest:
                source = (inv_sm[d] - seg_sm[N_DP + s // 2] + N_DP) % N_DP
                more = rrecv[r][source, HALF:]
            if d:
                fsend[r, d, :HALF] = tile
                if rest:
                    fsend[r, d, HALF:] = more
                for cp in f_copies(r, d, s):
                    cp.start()
            else:
                places = f_places(r, s)
                places[0][...] = tile
                if rest:
                    places[1][...] = more

    def o_part(r, owner):
        begin = pl.multiple_of((2 * owner + r // 2) * BLK, BLK)
        return out.at[pl.ds(r % 2 * HALF, HALF), pl.ds(begin, BLK)]

    def o_copy(r, o, owner, peer):
        return remote(osend.at[r, o], o_part(r, owner), o_send.at[r], o_recv.at[r], seq=peer)

    def o_own(r):
        return pltpu.make_async_copy(osend.at[r, 0], o_part(r, me), own_sem.at[ROUNDS + r])

    def send_seq(r):
        all_of(zsend.at[r], z_recv.at[r], N_DP - 1).wait()
        all_of(fsend.at[r], f_recv.at[r], N_DP - 1).wait()
        for o in ORDER:
            peer = seq_peer(y, x, c, o)
            osend[r, o] = zrecv[r][pick_sm[peer]]
            o_copy(r, o, me, peer).start()
        osend[r, 0] = zrecv[r][pick_sm[me]]
        o_own(r).start()

    def gather_drain():
        for half in range(2):
            for d in range(4):
                sib_copy(half, d).wait_send()
            for d in NEAR:
                ph1_copy(half, d, y if half else x).wait_send()
                for p in range(4):
                    ph2_copy(half, d, p).wait_send()

    def dp_drain(r):
        for ref, sem in ((zsend, z_send), (rsend, r_send), (fsend, f_send)):
            all_of(ref.at[r], sem.at[r], N_DP - 1).wait()

    def o_drain(r):
        o_own(r).wait()
        all_of(osend.at[r], o_send.at[r]).wait()
        all_of(osend.at[r], o_recv.at[r]).wait()

    for r in range(ROUNDS):
        q_arrive(r)
        attend(r)
        if r:
            forward(r - 1)
        send_relays(r)
        send_dp(r)
        if r == 0:
            q_start(2)
            q_start(3)
    gather_drain()
    send_seq(0)
    forward(ROUNDS - 1)
    for r in range(ROUNDS):
        q_drain(r)
    send_seq(1)
    o_drain(0)
    send_seq(2)
    dp_drain(0)
    dp_drain(1)
    o_drain(1)
    send_seq(3)
    dp_drain(2)
    dp_drain(3)
    o_drain(2)
    o_drain(3)


def call(relayed, index):
    bf16 = jnp.bfloat16
    piece = HALF + (relayed - N_DP) * HALF // N_DP
    vmem = pl.BlockSpec(memory_space=pltpu.VMEM)
    smem = pl.BlockSpec(memory_space=pltpu.SMEM)
    anywhere = pl.BlockSpec(memory_space=pl.ANY)
    dma = pltpu.SemaphoreType.DMA
    return pl.pallas_call(
        functools.partial(kernel, relayed),
        out_shape=jax.ShapeDtypeStruct((BLK, N_SEQ * 2 * HD_V), bf16),
        in_specs=[anywhere, vmem, vmem, vmem, vmem, smem, smem, smem],
        out_specs=anywhere,
        scratch_shapes=[
            *[pltpu.VMEM((NX, NC, HALF, XW), bf16)] * 8,
            pltpu.VMEM((2, NBLK, HALF, 2 * BLK), bf16),
            pltpu.VMEM((2, NBLK, HALF, BLK), bf16),
            pltpu.VMEM((LAT, 5 * BLK), bf16),
            pltpu.VMEM((2, LEAD + NBLK * BLK, 2 * BLK), bf16),
            pltpu.VMEM((2, LEAD + NBLK * BLK, 2 * BLK), bf16),
            pltpu.VMEM((ROUNDS, NBLK, HALF, BLK), bf16),
            pltpu.VMEM((ROUNDS, N_DP, DIRECT, HALF, BLK), bf16),
            *[pltpu.VMEM((N_DP * DIRECT + relayed, HALF, BLK), bf16)] * ROUNDS,
            pltpu.VMEM((ROUNDS, N_DP, piece, BLK), bf16),
            *[pltpu.VMEM((N_DP, piece, BLK), bf16)] * ROUNDS,
            pltpu.VMEM((ROUNDS, N_DP, piece, BLK), bf16),
            pltpu.VMEM((ROUNDS, N_SEQ, HALF, BLK), bf16),
            *[pltpu.SMEM((n,), jnp.int32)
              for n in (N_DP, NBLK, NBLK, N_DP, N_DP, relayed, relayed, N_DP)],
            dma((2, 4)), dma((2, 4)), dma((2, 4, 4)), dma((2, 4, 4)), dma((2, 4)), dma((2, 4)),
            dma((ROUNDS,)), dma((ROUNDS,)),
            dma((ROUNDS,)), dma((ROUNDS,)),
            dma((ROUNDS,)), dma((ROUNDS,)),
            dma((ROUNDS,)), dma((ROUNDS,)),
            dma((ROUNDS,)), dma((ROUNDS,)),
            dma((2 * ROUNDS,)),
        ],
        compiler_params=pltpu.CompilerParams(
            collective_id=index, has_side_effects=True, vmem_limit_bytes=56 * 2**20
        ),
    )


def on_device(queries, kv_latent, key_rope, kv_gain, kv_up, segment_blocks, bucket_of, doc_breaks):
    over = jnp.sum(jnp.maximum(segment_blocks - DIRECT, 0))
    return lax.cond(
        over <= RELAYS[0], call(RELAYS[0], 0), call(RELAYS[1], 1),
        queries, kv_latent, key_rope.T, kv_gain.reshape(1, LAT), kv_up, segment_blocks, bucket_of, doc_breaks,
    )


def solution(mesh):
    in_specs = (
        P(("dp", "seq"), None),
        P(("dp", "seq"), None),
        P(("dp", "seq"), None),
        P(),
        P(None, "seq"),
        P(),
        P(),
        P(),
    )
    return jax.shard_map(
        on_device, mesh=mesh, in_specs=in_specs, out_specs=P(("dp", "seq"), None), check_vma=False
    )
```
